512 devices in a mesh: gx: 16 (over z), gy: 8 (over x, core), gz: 4 (over y).
Axes of the slice: x: 4, y: 4, z: 16, core: 2. Of those that a mesh axis runs over, the one named last changes fastest.
Arguments:
- populations: float32 [19, 64, 64, 512], P(None, 'gx', 'gy', 'gz'), may hold values from 0.02 to 0.09
- solid_cells: int32 [64, 64, 512], P('gx', 'gy', 'gz'), may hold values 0 or 1
- slot_cells: int32 [16, 8, 4, 64, 8, 128], P('gx', 'gy', 'gz'), may hold values from 0 to 4095
- slot_weights: float32 [16, 8, 4, 64, 8, 128], P('gx', 'gy', 'gz'), may hold values from 0 to 0.0625
- slot_owner: int32 [16, 8, 4, 64, 1], P('gx', 'gy', 'gz'), may hold values from 0 to 127; in each aligned block of 64 rows (0 to 63, 64 to 127, ..., all dimensions but the last counted through in order) at most 2 rows name the same one
- slot_block: int32 [16, 8, 4, 64], P('gx', 'gy', 'gz'), may hold values from 0 to 31
- train_of_block: int32 [16, 8, 4, 32], P('gx', 'gy', 'gz'), may hold values from 0 to 3
- marker_area: float32 [16, 8, 4, 32, 128], P('gx', 'gy', 'gz'), may hold values from 0.5 to 2
- train_velocity: float32 [4, 3], replicated, may hold values from -0.1 to 0.1
Outputs:
- populations_next: float32 [19, 64, 64, 512], P(None, 'gx', 'gy', 'gz')
- marker_force: float32 [16, 8, 4, 32, 3, 128], P('gx', 'gy', 'gz')
The draws below stay inside these ranges and needn't reach their ends.
Inputs may be any that keep to these rules, and one draw needn't show every extreme that they name: `slot_owner`: among the 64 slots of one device no owner is named more than 2 times, a bound that some block reaches.
All inputs are finite; a program needn't handle non-finite values. No bound on the sum of `solid_cells` on one device may be relied on, other than what follows from the above.
Results may differ from the reference program's by a relative error of at most 0.000065.
Values sent between devices are 32-bit elements; how exact they have to be, the bound alone decides.
A program may use at most 128 MiB of HBM per device.

```python
import math
import jax
import jax.numpy as jnp
import numpy as np
from jax import lax

CX = 4
CY = 8
CZ = 128
SLOTS = 64
OWN = 32
MARK = 128
KERN = 8
TRAINS = 4
CAP = 2
NX = 64
NY = 64
NZ = 512
N_GX = 16
N_GY = 8
N_GZ = 4


def set_ends(entries, rng, least, top_value):
    shape = entries.shape
    index_at = [jax.random.randint(jax.random.fold_in(rng, axis), (), 0, shape[axis]) for axis in range(len(shape))]
    entries = entries.at[tuple(index_at)].set(least)
    longest = shape.index(max(shape))
    index_at[longest] = (index_at[longest] + 1) % shape[longest]
    return entries.at[tuple(index_at)].set(top_value)


def level_of(stream_key, dims, pieces, least, largest):
    loudness = 1.0
    for dim, shards_of in pieces:
        heights = jax.random.uniform(jax.random.fold_in(jax.random.fold_in(stream_key, 6), dim), (shards_of,), jnp.float32, least / len(pieces), largest / len(pieces))
        loudness = loudness * jnp.repeat(jnp.exp(heights), dims[dim] // shards_of).reshape((-1,) + (1,) * (len(dims) - 1 - dim))
    return loudness


def deal_out(rng, own, number, rows, amount, top, most, slope):
    ranking = jax.random.permutation(rng, amount)
    heavy_load, usual = portions_of(amount, rows * top, most, slope, True), portions_of(amount, rows * top, most, slope, False)
    places = jnp.arange(amount)

    def named(tallies, rotation):
        used = int((tallies > 0).sum())
        fixed = max(1, used // 4)
        shifted = fixed + (places - fixed + rotation * (used - fixed)) % max(1, amount - fixed)
        return jnp.zeros((amount,), jnp.int32).at[ranking[jnp.where(places < fixed, places, shifted)]].set(jnp.asarray(tallies, jnp.int32))

    tallies = jnp.where(number % 4 == 0, named(heavy_load, number // 4), named(usual, number - number // 4 - 1))
    mixed = jax.random.permutation(jax.random.fold_in(own, 3), amount)
    source_of, taker = mixed[0:amount // 2 * 2:2], mixed[1:amount // 2 * 2:2]
    slack = jnp.minimum(tallies[source_of] - 1, most - tallies[taker]) // 2
    slack = jnp.where((source_of == ranking[0]) | (taker == ranking[0]) | (tallies[taker] == 0), 0, jnp.maximum(slack, 0))
    shifted = jax.random.randint(jax.random.fold_in(own, 4), (amount // 2,), 0, 1 << 20) % (slack + 1)
    tallies = tallies.at[source_of].add(-shifted).at[taker].add(shifted)
    items = jnp.searchsorted(jnp.cumsum(tallies), jnp.arange(rows * top), side="right").astype(jnp.int32)
    listing = items.reshape(top, rows).T
    listing = listing[jax.random.permutation(jax.random.fold_in(own, 1), rows)]
    rotation = jax.random.randint(jax.random.fold_in(own, 2), (rows, 1), 0, top)
    return jnp.take_along_axis(listing, (jnp.arange(top)[None, :] + rotation) % top, axis=1)


def portions_of(amount, total, most, skew, full):
    portions = [(1 << 20) // math.isqrt(grade ** skew) + 1 for grade in range(1, amount + 1)]
    largest = most if full else min(most, max(-(-total // amount), total * portions[0] // sum(portions)))
    least = 1 if total - largest >= amount - 1 else 0
    holding, spare = [largest] + [least] * (amount - 1), total - largest - least * (amount - 1)
    while spare > 0:
        movable = [i for i in range(1, amount) if holding[i] < largest] or [i for i in range(1, amount) if holding[i] < most]
        mass, left = sum([portions[i] for i in movable]), spare
        for i in movable:
            more = min(most - holding[i], max(1, left * portions[i] // mass), spare)
            holding[i] = holding[i] + more
            spare = spare - more
    return np.array(holding)


def setup_inputs(seed: int = 0) -> dict:
    seeds = jax.random.split(jax.random.key(seed), 10)
    populations = jnp.clip(0.02 + 0.07000000402331352 * jax.random.uniform(seeds[0], (19, NX, NY, NZ), jnp.float32) ** level_of(seeds[0], (19, NX, NY, NZ), ((1, 16), (2, 8), (3, 4)), -0.2, 0.2), 0.02, 0.09)
    solid_cells = set_ends((jax.random.randint(seeds[1], (NX, NY, NZ), 0, 8) < 1).astype(jnp.int32), jax.random.fold_in(seeds[1], 1), 0, 1)
    slot_cells = set_ends(jax.random.randint(seeds[2], (N_GX, N_GY, N_GZ, SLOTS, KERN, MARK), 0, min(CX * CY * CZ, 16369)), jax.random.fold_in(seeds[2], 1), 0, (min(CX * CY * CZ, 16369)) - 1).astype(jnp.int32)
    slot_weights = jnp.clip(0.0625 * jax.random.uniform(seeds[3], (N_GX, N_GY, N_GZ, SLOTS, KERN, MARK), jnp.float32) ** level_of(seeds[3], (N_GX, N_GY, N_GZ, SLOTS, KERN, MARK), ((0, 16), (1, 8), (2, 4)), -0.2, 0.2), 0.0, 0.0625)
    slot_owner_keys = jax.random.split(jax.random.fold_in(seeds[4], 1), N_GX * N_GY * N_GZ * SLOTS // SLOTS)
    slot_owner_turns = jax.random.permutation(jax.random.fold_in(seeds[4], 3), N_GX * N_GY * N_GZ * SLOTS // SLOTS)
    slot_owner = jax.vmap(lambda own, number: deal_out(jax.random.fold_in(seeds[4], 2), own, number, SLOTS, N_GX * N_GY, 1, CAP, 2))(slot_owner_keys, slot_owner_turns).reshape((N_GX, N_GY, N_GZ, SLOTS, 1))
    slot_block = set_ends(jax.random.randint(seeds[5], (N_GX, N_GY, N_GZ, SLOTS), 0, OWN), jax.random.fold_in(seeds[5], 1), 0, OWN - 1).astype(jnp.int32)
    train_of_block = set_ends(jax.random.randint(seeds[6], (N_GX, N_GY, N_GZ, OWN), 0, TRAINS), jax.random.fold_in(seeds[6], 1), 0, TRAINS - 1).astype(jnp.int32)
    marker_area = jnp.clip(jnp.exp(math.log(2.0) - 1.3862944 * jax.random.uniform(seeds[7], (N_GX, N_GY, N_GZ, OWN, MARK), jnp.float32) ** level_of(seeds[7], (N_GX, N_GY, N_GZ, OWN, MARK), ((0, 16), (1, 8), (2, 4)), -0.2, 0.2)), 0.5, 2.0)
    train_velocity = jnp.clip(jax.random.uniform(seeds[8], (TRAINS, 3), jnp.float32, -0.1, 0.1), -0.1, 0.1)
    return dict(populations=populations, solid_cells=solid_cells, slot_cells=slot_cells, slot_weights=slot_weights, slot_owner=slot_owner, slot_block=slot_block, train_of_block=train_of_block, marker_area=marker_area, train_velocity=train_velocity)


velocity_table = np.array([[0, 0, 0], [1, 0, 0], [-1, 0, 0], [0, 1, 0], [0, -1, 0], [0, 0, 1], [0, 0, -1], [1, 1, 0], [-1, -1, 0], [1, -1, 0], [-1, 1, 0], [1, 0, 1], [-1, 0, -1], [1, 0, -1], [-1, 0, 1], [0, 1, 1], [0, -1, -1], [0, 1, -1], [0, -1, 1]])
weight_table = [1.0 / 3.0] + [1.0 / 18.0] * 6 + [1.0 / 36.0] * 12
opposite_table = [0, 2, 1, 4, 3, 6, 5, 8, 7, 10, 9, 12, 11, 14, 13, 16, 15, 18, 17]
stress_pairs = [(0, 0), (1, 1), (2, 2), (0, 1), (0, 2), (1, 2)]
tau_base = 0.55
smag_term = 18.0 * 1.4142135623730951 * 0.17 * 0.17
regular_eps = 0.0001
stiffness = 2.0
far_velocity = (0.02, 0.06, 0.0)

def project(direction, vector):
    projection = 0.0 * vector[0]
    for component in range(3):
        lattice_step = int(velocity_table[direction][component])
        if lattice_step != 0:
            projection = projection + lattice_step * vector[component]
    return projection

def moments(populations):
    density = populations[0]
    momentum = [jnp.zeros_like(density) for component in range(3)]
    for direction in range(1, 19):
        density = density + populations[direction]
        for component in range(3):
            lattice_step = int(velocity_table[direction][component])
            if lattice_step == 1:
                momentum[component] = momentum[component] + populations[direction]
            elif lattice_step == -1:
                momentum[component] = momentum[component] - populations[direction]
    return (density, momentum)

def equilibrium(density, velocity):
    speed_sq = velocity[0] * velocity[0] + velocity[1] * velocity[1] + velocity[2] * velocity[2]
    result = []
    for direction in range(19):
        projected = project(direction, velocity)
        result.append(weight_table[direction] * density * (1.0 + 3.0 * projected + 4.5 * projected * projected - 1.5 * speed_sq))
    return result

def collide(populations, cell_force, solid_cells):
    density, momentum = moments(populations)
    velocity = [(momentum[component] + 0.5 * cell_force[component]) / density for component in range(3)]
    balance = equilibrium(density, velocity)
    stress = [jnp.zeros_like(density) for pair_pos in range(6)]
    for direction in range(19):
        non_eq = populations[direction] - balance[direction]
        for pair_pos in range(6):
            row_axis, col_axis = stress_pairs[pair_pos]
            factor = int(velocity_table[direction][row_axis] * velocity_table[direction][col_axis])
            if factor != 0:
                stress[pair_pos] = stress[pair_pos] + factor * non_eq
    shear_sq = stress[0] * stress[0] + stress[1] * stress[1] + stress[2] * stress[2]
    shear_sq = shear_sq + 2.0 * (stress[3] * stress[3] + stress[4] * stress[4] + stress[5] * stress[5])
    magnitude = jnp.sqrt(shear_sq + regular_eps)
    relax_time = 0.5 * (tau_base + jnp.sqrt(tau_base * tau_base + smag_term * magnitude / density))
    guo_factor = 1.0 - 0.5 / relax_time
    speed_force = velocity[0] * cell_force[0] + velocity[1] * cell_force[1] + velocity[2] * cell_force[2]
    result = []
    for direction in range(19):
        along_force = project(direction, cell_force)
        along_speed = project(direction, velocity)
        source = guo_factor * weight_table[direction] * (3.0 * (along_force - speed_force) + 9.0 * along_speed * along_force)
        relaxed = populations[direction] - (populations[direction] - balance[direction]) / relax_time + source
        result.append(jnp.where(solid_cells == 1, populations[opposite_table[direction]], relaxed))
    return jnp.stack(result)

def reference(populations, solid_cells, slot_cells, slot_weights, slot_owner, slot_block, train_of_block, marker_area, train_velocity):
    density, momentum = moments(populations)
    rest_velocity = jnp.stack([momentum[component] / density for component in range(3)])
    cell_count = CX * CY * CZ
    tile_velocity = rest_velocity.reshape(3, N_GX, CX, N_GY, CY, N_GZ, CZ).transpose(1, 3, 5, 0, 2, 4, 6)
    tile_velocity = tile_velocity.reshape(N_GX, N_GY, N_GZ, 3, cell_count)

    def sample_tile(velocity_tile, cells_tile, weight_tile):
        return lax.optimization_barrier(jnp.sum(velocity_tile[:, cells_tile] * weight_tile[None], axis=2))

    def sample_plane(inputs):
        return jax.vmap(jax.vmap(sample_tile))(inputs[0], inputs[1], inputs[2])
    partial_value = lax.map(sample_plane, (tile_velocity, slot_cells, slot_weights))
    slot_rows = partial_value.transpose(0, 1, 2, 4, 3, 5).reshape(-1, 3 * MARK)
    layer = jnp.arange(N_GZ, dtype=jnp.int32)[None, None, :, None]
    block_id = ((slot_owner[..., 0] * N_GZ + layer) * OWN + slot_block).reshape(-1).astype(jnp.int32)
    marker_velocity = jax.ops.segment_sum(slot_rows, block_id, num_segments=N_GX * N_GY * N_GZ * OWN)
    marker_velocity = marker_velocity.reshape(N_GX, N_GY, N_GZ, OWN, 3, MARK)
    target = train_velocity[train_of_block]
    marker_force = stiffness * marker_area[..., None, :] * (target[..., None] - marker_velocity)
    slot_force = marker_force.reshape(-1, 3 * MARK)[block_id].reshape(N_GX, N_GY, N_GZ, SLOTS, 3, MARK)

    def spread_tile(force_tile, cells_tile, weight_tile):
        contrib = weight_tile[None] * force_tile.transpose(1, 0, 2)[:, :, None, :]
        return jnp.zeros((3, cell_count), jnp.float32).at[:, cells_tile.reshape(-1)].add(contrib.reshape(3, -1))

    def spread_plane(inputs):
        return jax.vmap(jax.vmap(spread_tile))(inputs[0], inputs[1], inputs[2])
    force_tiles = lax.map(spread_plane, (slot_force, slot_cells, slot_weights))
    cell_force = force_tiles.reshape(N_GX, N_GY, N_GZ, 3, CX, CY, CZ).transpose(3, 0, 4, 1, 5, 2, 6).reshape(3, NX, NY, NZ)
    relaxed = collide(populations, cell_force, solid_cells)
    read = jnp.stack([jnp.roll(relaxed[direction], tuple((int(lattice_step) for lattice_step in velocity_table[direction])), axis=(0, 1, 2)) for direction in range(19)])
    global_y = jnp.arange(NY, dtype=jnp.int32)
    global_z = jnp.arange(NZ, dtype=jnp.int32)
    on_side = ((global_y == 0) | (global_y == NY - 1))[:, None] | ((global_z == 0) | (global_z == NZ - 1))[None, :]
    far_field = jnp.array(equilibrium(1.0, list(far_velocity)), dtype=jnp.float32)
    populations_next = jnp.where(on_side[None, None], far_field[:, None, None, None], read)
    return (populations_next, marker_force)
```

```python
import functools

import jax
import jax.numpy as jnp
import numpy as np
from jax import lax
from jax.experimental import pallas as pl
from jax.experimental.pallas import tpu as pltpu
from jax.sharding import PartitionSpec as P

velocity_table = np.array(
    [
        [0, 0, 0],
        [1, 0, 0],
        [-1, 0, 0],
        [0, 1, 0],
        [0, -1, 0],
        [0, 0, 1],
        [0, 0, -1],
        [1, 1, 0],
        [-1, -1, 0],
        [1, -1, 0],
        [-1, 1, 0],
        [1, 0, 1],
        [-1, 0, -1],
        [1, 0, -1],
        [-1, 0, 1],
        [0, 1, 1],
        [0, -1, -1],
        [0, 1, -1],
        [0, -1, 1],
    ]
)
weight_table = [1.0 / 3.0] + [1.0 / 18.0] * 6 + [1.0 / 36.0] * 12
opposite_table = [0, 2, 1, 4, 3, 6, 5, 8, 7, 10, 9, 12, 11, 14, 13, 16, 15, 18, 17]
stress_pairs = [(0, 0), (1, 1), (2, 2), (0, 1), (0, 2), (1, 2)]
tau_base = 0.55
smag_term = 18.0 * 1.4142135623730951 * 0.17 * 0.17
regular_eps = 0.0001
stiffness = 2.0
far_velocity = (0.02, 0.06, 0.0)
MESH = pl.DeviceIdType.MESH
f32 = jnp.float32
bf16 = jnp.bfloat16
i32 = jnp.int32

facing = [
    {sign: [q for q in range(19) if velocity_table[q][axis] == sign] for sign in (1, -1)}
    for axis in range(3)
]
Z_SIDES = ((0, 0), (1, 0), (-1, 0), (0, 1), (0, -1))
Y_SIDES = (0, 1, -1)


def project(direction, vector):
    projection = None
    for component in range(3):
        lattice_step = int(velocity_table[direction][component])
        if lattice_step != 0:
            term = vector[component] if lattice_step == 1 else -vector[component]
            projection = term if projection is None else projection + term
    return projection


def moments(populations):
    density = populations[0]
    momentum = [None, None, None]
    for direction in range(1, 19):
        density = density + populations[direction]
        for component in range(3):
            lattice_step = int(velocity_table[direction][component])
            if lattice_step != 0:
                term = populations[direction] if lattice_step == 1 else -populations[direction]
                momentum[component] = (
                    term if momentum[component] is None else momentum[component] + term
                )
    return (density, momentum)


def equilibrium(density, velocity):
    speed_sq = velocity[0] * velocity[0] + velocity[1] * velocity[1] + velocity[2] * velocity[2]
    base = 1.0 - 1.5 * speed_sq
    result = []
    for direction in range(19):
        projected = project(direction, velocity)
        inner = base if projected is None else base + projected * (3.0 + 4.5 * projected)
        result.append(weight_table[direction] * density * inner)
    return result


def far_field():
    speed_sq = sum(v * v for v in far_velocity)
    values = []
    for direction in range(19):
        projected = sum(int(velocity_table[direction][i]) * far_velocity[i] for i in range(3))
        values.append(
            weight_table[direction]
            * (1.0 + 3.0 * projected + 4.5 * projected * projected - 1.5 * speed_sq)
        )
    return values


def collide(populations, cell_force, solid):
    density, momentum = moments(populations)
    inverse = 1.0 / density
    velocity = [
        (momentum[component] + 0.5 * cell_force[component]) * inverse for component in range(3)
    ]
    balance = equilibrium(density, velocity)
    stress = [None] * 6
    departure = []
    for direction in range(19):
        non_eq = populations[direction] - balance[direction]
        departure.append(non_eq)
        for pair_pos in range(6):
            row_axis, col_axis = stress_pairs[pair_pos]
            factor = int(velocity_table[direction][row_axis] * velocity_table[direction][col_axis])
            if factor != 0:
                term = non_eq if factor == 1 else -non_eq
                stress[pair_pos] = term if stress[pair_pos] is None else stress[pair_pos] + term
    shear_sq = stress[0] * stress[0] + stress[1] * stress[1] + stress[2] * stress[2]
    shear_sq = shear_sq + 2.0 * (
        stress[3] * stress[3] + stress[4] * stress[4] + stress[5] * stress[5]
    )
    magnitude = jnp.sqrt(shear_sq + regular_eps)
    relax_time = 0.5 * (tau_base + jnp.sqrt(tau_base * tau_base + smag_term * magnitude * inverse))
    rate = 1.0 / relax_time
    guo_factor = 1.0 - 0.5 * rate
    speed_force = (
        velocity[0] * cell_force[0] + velocity[1] * cell_force[1] + velocity[2] * cell_force[2]
    )
    base = -3.0 * speed_force
    result = []
    for direction in range(19):
        along_force = project(direction, cell_force)
        along_speed = project(direction, velocity)
        inner = base if along_force is None else base + along_force * (3.0 + 9.0 * along_speed)
        relaxed = (
            populations[direction]
            - departure[direction] * rate
            + (guo_factor * weight_table[direction]) * inner
        )
        result.append(jnp.where(solid, populations[opposite_table[direction]], relaxed))
    return result


def pick_rows(one_hot, values):
    high = values.astype(bf16)
    rest = values - high.astype(f32)
    middle = rest.astype(bf16)
    low = (rest - middle.astype(f32)).astype(bf16)
    total = jnp.dot(one_hot, low, preferred_element_type=f32)
    total = total + jnp.dot(one_hot, middle, preferred_element_type=f32)
    return total + jnp.dot(one_hot, high, preferred_element_type=f32)


def iota(shape, dim):
    return lax.broadcasted_iota(i32, shape, dim)


def hot(condition):
    return jnp.where(condition, 1.0, 0.0).astype(bf16)


def to_column(row):
    n = row.shape[1]
    square = jnp.broadcast_to(row, (n, n))
    return jnp.sum(jnp.where(iota((n, n), 0) == iota((n, n), 1), square, 0.0), axis=1, keepdims=True)


def kernel(
    px,
    py,
    pz,
    pop,
    solid,
    cells,
    weights,
    owner,
    block,
    train,
    area,
    speed,
    out,
    force_out,
    table,
    rows,
    place,
    place_t,
    combine,
    combine_t,
    lab_send,
    lab_recv,
    z_send,
    z_recv,
    d_send,
    d_recv,
    f_all,
    r_send,
    r_recv,
    lane_hot,
    cell_force,
    relaxed,
    x_send,
    x_recv,
    y_send,
    y_recv,
    t_send,
    t_recv,
    send_sem,
    recv_sem,
    halo_send,
    halo_recv,
):
    slots, kern, mark = cells.shape
    size_x, size_y, size_z = pop.shape[1:]
    own = area.shape[0]
    cap = 2
    per_plane = py * cap
    total_rows = px * per_plane
    row_count = size_x * size_y
    gx, gy, gz = lax.axis_index("gx"), lax.axis_index("gy"), lax.axis_index("gz")

    def at(dx, dy, dz):
        return (
            lax.rem(gx + px + dx, px),
            lax.rem(gy + py + dy, py),
            lax.rem(gz + pz + dz, pz),
        )

    halo_far = (
        [(0, 0, s) for s in (1, -1)]
        + [(a, b, 0) for a in (1, -1) for b in (1, -1)]
        + [(a, 0, b) for a in (1, -1) for b in (1, -1)]
        + [(0, a, b) for a in (1, -1) for b in (1, -1)]
    )
    barrier = pltpu.get_barrier_semaphore()

    def greet_x(k, _):
        pl.semaphore_signal(barrier, inc=1, device_id=at(k, 0, 0), device_id_type=MESH)
        return 0

    def greet_y(k, _):
        pl.semaphore_signal(barrier, inc=1, device_id=at(0, k, 0), device_id_type=MESH)
        return 0

    lax.fori_loop(1, px, greet_x, 0)
    lax.fori_loop(1, py, greet_y, 0)
    for place_of in halo_far:
        pl.semaphore_signal(barrier, inc=1, device_id=at(*place_of), device_id_type=MESH)

    owner_row = owner[...].astype(f32)
    owner_col = to_column(owner_row)
    same = owner_col == owner_row
    first, second = iota((slots, slots), 0), iota((slots, slots), 1)
    rank_row = jnp.sum(jnp.where(same & (first < second), 1.0, 0.0), axis=0, keepdims=True)
    rank_col = jnp.sum(jnp.where(same & (second < first), 1.0, 0.0), axis=1, keepdims=True)
    target_row = (owner_row * cap + rank_row).astype(i32)
    target_col = (owner_col * cap + rank_col).astype(i32)
    place[...] = hot(iota((total_rows, slots), 0) == target_row)
    place_t[...] = hot(iota((slots, total_rows), 1) == target_col)
    label_col = to_column(block[...].astype(f32)) + 1.0
    half = mark // per_plane
    plane_hot = hot(iota((px, slots), 0) == target_row // per_plane)
    spot = lax.rem(target_col, per_plane) + per_plane * lax.rem(gx, half)
    label_hot = jnp.where(iota((slots, mark), 1) == spot, label_col, 0.0).astype(bf16)
    labels = jnp.dot(plane_hot, label_hot, preferred_element_type=f32)
    lab_send[...] = jnp.broadcast_to(labels[:, None, :], lab_send.shape)
    lab_recv[gx] = lab_send[gx]

    density, momentum = moments([pop[q] for q in range(19)])
    for c in range(3):
        table[c] = (momentum[c] / density).reshape(row_count, size_z)

    pl.semaphore_wait(barrier, px - 1 + py - 1 + len(halo_far))

    def send_x(source, target, stage):
        def step(i, _):
            k = px // 2 + ((i + 1) // 2) * (1 - 2 * lax.rem(i, 2))
            peer = at(k, 0, 0)
            pltpu.make_async_remote_copy(
                src_ref=source.at[peer[0]],
                dst_ref=target.at[gx],
                send_sem=send_sem.at[stage],
                recv_sem=recv_sem.at[stage],
                device_id=peer,
                device_id_type=MESH,
            ).start()
            return 0

        lax.fori_loop(0, px - 1, step, 0)

    def send_y(source, own_place, target, stage):
        def step(k, _):
            peer = at(0, k, 0)
            pltpu.make_async_remote_copy(
                src_ref=source.at[gy if own_place else peer[1]],
                dst_ref=target.at[gy],
                send_sem=send_sem.at[stage],
                recv_sem=recv_sem.at[stage],
                device_id=peer,
                device_id_type=MESH,
            ).start()
            return 0

        lax.fori_loop(1, py, step, 0)

    def wait_for(buffer, count, semaphore):
        part = buffer.at[pl.ds(0, count)]
        pltpu.make_async_copy(part, part, semaphore).wait()

    LAB, ZS, DS, FS, RS = 0, 1, 4, 7, 10
    send_x(lab_send, lab_recv, LAB)

    def gather(c, begin, end):
        def step(s, _):
            index = cells[s]
            lane = index & (size_z - 1)
            line = index // size_z
            found = jnp.zeros((kern, mark), f32)
            for h in range(row_count):
                entry = jnp.broadcast_to(table[c, h : h + 1, :], (kern, size_z))
                found = jnp.where(line == h, jnp.take_along_axis(entry, lane, axis=1), found)
            rows[c, pl.ds(s, 1), :] = jnp.sum(found * weights[s], axis=0, keepdims=True)
            return 0

        lax.fori_loop(begin, end, step, 0)

    def send_rows(c):
        z_send[c] = pick_rows(place[...], rows[c]).reshape(px, per_plane, mark)
        z_recv[c, gx] = z_send[c, gx]
        send_x(z_send.at[c], z_recv.at[c], ZS + c)

    def read_labels():
        wait_for(lab_recv, px - 1, recv_sem.at[LAB])
        parts, columns = [], []
        for n in range(total_rows // mark):
            label = jnp.sum(lab_recv[n * half : (n + 1) * half], axis=0)[0:1]
            group = lax.rem(iota((1, mark), 1), per_plane) // cap
            key = jnp.where(label > 0.5, group.astype(f32) * own + label - 1.0, -1.0)
            parts.append(key)
            columns.append(to_column(key))
        key_row = jnp.concatenate(parts, axis=1).astype(i32)
        key_col = jnp.concatenate(columns, axis=0).astype(i32)
        combine[...] = hot(iota((py * own, total_rows), 0) == key_row)
        combine_t[...] = hot(iota((total_rows, py * own), 1) == key_col)

    def send_sums(c):
        wait_for(z_recv.at[c], px - 1, recv_sem.at[ZS + c])
        d_send[c] = pick_rows(combine[...], z_recv[c].reshape(total_rows, mark)).reshape(
            py, own, mark
        )
        d_recv[c, gy] = d_send[c, gy]
        send_y(d_send.at[c], False, d_recv.at[c], DS + c)

    train_col = to_column(train[...].astype(f32))

    def send_force(c):
        wait_for(d_recv.at[c], py - 1, recv_sem.at[DS + c])
        marker_velocity = d_recv[c, 0]
        for n in range(1, py):
            marker_velocity = marker_velocity + d_recv[c, n]
        goal = jnp.zeros((own, 1), f32)
        for t in range(speed.shape[0]):
            goal = jnp.where(train_col == float(t), speed[t, c], goal)
        force = stiffness * area[...] * (goal - marker_velocity)
        force_out[:, c, :] = force
        f_all[c, gy] = force
        send_y(f_all.at[c], True, f_all.at[c], FS + c)

    def send_back(c):
        wait_for(f_all.at[c], py - 1, recv_sem.at[FS + c])
        r_send[c] = pick_rows(combine_t[...], f_all[c].reshape(py * own, mark)).reshape(
            px, per_plane, mark
        )
        r_recv[c, gx] = r_send[c, gx]
        send_x(r_send.at[c], r_recv.at[c], RS + c)

    def lane_one_hots(begin, end):
        def step(s, _):
            lane = (cells[s] & (size_z - 1)).astype(f32)
            for k in range(kern):
                wanted = jnp.broadcast_to(lane[k : k + 1, :], (16, mark)).astype(bf16)
                for j in range(size_z // 16):
                    place_of = (iota((16, mark), 0) + 16 * j).astype(f32).astype(bf16)
                    lane_hot[s, 16 * j : 16 * j + 16, k * mark : (k + 1) * mark] = jnp.where(
                        wanted == place_of, bf16(1), bf16(0)
                    )
            return 0

        lax.fori_loop(begin, end, step, 0)

    def spread(c):
        wait_for(r_recv.at[c], px - 1, recv_sem.at[RS + c])
        rows[c] = pick_rows(place_t[...], r_recv[c].reshape(total_rows, mark))

        def step(s, total):
            line = (cells[s] // size_z).astype(f32)
            value = weights[s] * rows[c, pl.ds(s, 1), :]
            high = value.astype(bf16).astype(f32)
            low = value - high
            zero = bf16(0)
            columns = []
            for k in range(kern):
                wanted = jnp.broadcast_to(line[k : k + 1, :], (16, mark)).astype(bf16)
                pieces = []
                for piece in (high, low):
                    spread_piece = jnp.broadcast_to(piece[k : k + 1, :], (16, mark)).astype(bf16)
                    for j in range(row_count // 16):
                        place_of = (iota((16, mark), 0) + 16 * j).astype(f32).astype(bf16)
                        pieces.append(jnp.where(wanted == place_of, spread_piece, zero))
                columns.append(jnp.concatenate(pieces, axis=0))
            return total + lax.dot_general(
                jnp.concatenate(columns, axis=1),
                lane_hot[s],
                (((1,), (1,)), ((), ())),
                preferred_element_type=f32,
            )

        total = lax.fori_loop(0, slots, step, jnp.zeros((2 * row_count, size_z), f32))
        cell_force[c] = (total[:row_count] + total[row_count:]).reshape(size_x, size_y, size_z)

    gather(0, 0, slots)
    send_rows(0)
    gather(1, 0, slots)
    send_rows(1)
    read_labels()
    gather(2, 0, slots // 2)
    send_sums(0)
    gather(2, slots // 2, slots)
    send_rows(2)
    send_force(0)
    lane_one_hots(0, slots // 4)
    send_back(0)
    send_sums(1)
    lane_one_hots(slots // 4, slots // 2)
    send_force(1)
    lane_one_hots(slots // 2, 3 * slots // 4)
    send_back(1)
    send_sums(2)
    lane_one_hots(3 * slots // 4, slots)
    send_force(2)
    send_back(2)
    spread(0)
    spread(1)
    spread(2)

    def relax(x, _):
        result = collide(
            [pop[q, x] for q in range(19)], [cell_force[c, x] for c in range(3)], solid[x] == 1
        )
        for q in range(19):
            relaxed[q, x] = result[q]
        return 0

    lax.fori_loop(0, size_x, relax, 0)

    lane_at = iota((size_y, size_z), 1)
    line_at = iota((size_y, size_z), 0)
    halo = []

    def send_halo(source, target, place_of):
        n = len(halo)
        copy = pltpu.make_async_remote_copy(
            src_ref=source,
            dst_ref=target,
            send_sem=halo_send.at[n],
            recv_sem=halo_recv.at[n],
            device_id=at(*place_of),
            device_id_type=MESH,
        )
        copy.start()
        halo.append(copy)

    for d, sign in enumerate((1, -1)):
        tile = jnp.zeros((size_y, size_z), f32)
        edge = size_z - 1 if sign == 1 else 0
        for n, q in enumerate(facing[2][sign]):
            for x in range(size_x):
                column = jnp.broadcast_to(relaxed[q, x][:, edge : edge + 1], (size_y, size_z))
                tile = jnp.where(lane_at == n * size_x + x, column, tile)
        t_send[d] = tile
        for side, (dx, dy) in enumerate(Z_SIDES):
            send_halo(t_send.at[d], t_recv.at[d, side], (dx, dy, sign))
    for d, sign in enumerate((1, -1)):
        edge = size_y - 1 if sign == 1 else 0
        for n, q in enumerate(facing[1][sign]):
            y_send[d, n * size_x : (n + 1) * size_x, :] = relaxed[q, :, edge, :]
        for side, dx in enumerate(Y_SIDES):
            send_halo(y_send.at[d], y_recv.at[d, side], (dx, sign, 0))
    for d, sign in enumerate((1, -1)):
        edge = size_x - 1 if sign == 1 else 0
        for n, q in enumerate(facing[0][sign]):
            x_send[d, n] = relaxed[q, edge]
        send_halo(x_send.at[d], x_recv.at[d], (sign, 0, 0))
    for copy in halo:
        copy.wait_recv()

    on_side = (
        ((line_at == 0) & (gy == 0))
        | ((line_at == size_y - 1) & (gy == py - 1))
        | ((lane_at == 0) & (gz == 0))
        | ((lane_at == size_z - 1) & (gz == pz - 1))
    )
    far = far_field()
    for q in range(19):
        cx, cy, cz = (int(v) for v in velocity_table[q])
        for x in range(size_x):
            source = x - cx
            inside = 0 <= source < size_x
            at_edge = source % size_x
            if inside:
                plane = relaxed[q, source]
            else:
                plane = x_recv[0 if cx == 1 else 1, facing[0][cx].index(q)]
            side = 0 if inside else (1 if cx == 1 else 2)
            if cy != 0:
                d = 0 if cy == 1 else 1
                n = facing[1][cy].index(q) * size_x + at_edge
                row = jnp.broadcast_to(y_recv[d, side, n : n + 1, :], (size_y, size_z))
                plane = pltpu.roll(plane, cy % size_y, 0)
                plane = jnp.where(line_at == (0 if cy == 1 else size_y - 1), row, plane)
            if cz != 0:
                d = 0 if cz == 1 else 1
                n = facing[2][cz].index(q) * size_x + at_edge
                tile = t_recv[d, side]
                if cy != 0:
                    beside = pltpu.roll(t_recv[d, 3 if cy == 1 else 4], cy % size_y, 0)
                    tile = pltpu.roll(tile, cy % size_y, 0)
                    tile = jnp.where(line_at == (0 if cy == 1 else size_y - 1), beside, tile)
                column = jnp.broadcast_to(tile[:, n : n + 1], (size_y, size_z))
                plane = pltpu.roll(plane, cz % size_z, 1)
                plane = jnp.where(lane_at == (0 if cz == 1 else size_z - 1), column, plane)
            out[q, x] = jnp.where(on_side, f32(far[q]), plane)

    wait_for(lab_send, px - 1, send_sem.at[LAB])
    for c in range(3):
        wait_for(z_send.at[c], px - 1, send_sem.at[ZS + c])
        wait_for(d_send.at[c], py - 1, send_sem.at[DS + c])
        wait_for(f_all.at[c], py - 1, send_sem.at[FS + c])
        wait_for(r_send.at[c], px - 1, send_sem.at[RS + c])
    for copy in halo:
        copy.wait_send()


def per_device(
    populations,
    solid_cells,
    slot_cells,
    slot_weights,
    slot_owner,
    slot_block,
    train_of_block,
    marker_area,
    train_velocity,
):
    px, py, pz = (lax.axis_size(axis) for axis in ("gx", "gy", "gz"))
    slots, kern, mark = slot_cells.shape[3:]
    own = train_of_block.shape[3]
    _, size_x, size_y, size_z = populations.shape
    rows_out = px * py * 2
    vmem = pl.BlockSpec(memory_space=pltpu.VMEM)
    smem = pl.BlockSpec(memory_space=pltpu.SMEM)
    face = 5 * size_x
    face_rows = -(-face // 8) * 8
    scratch = [
        pltpu.VMEM((3, size_x * size_y, size_z), f32),
        pltpu.VMEM((3, slots, mark), f32),
        pltpu.VMEM((rows_out, slots), bf16),
        pltpu.VMEM((slots, rows_out), bf16),
        pltpu.VMEM((py * own, rows_out), bf16),
        pltpu.VMEM((rows_out, py * own), bf16),
        pltpu.VMEM((px, 8, mark), f32),
        pltpu.VMEM((px, 8, mark), f32),
        pltpu.VMEM((3, px, py * 2, mark), f32),
        pltpu.VMEM((3, px, py * 2, mark), f32),
        pltpu.VMEM((3, py, own, mark), f32),
        pltpu.VMEM((3, py, own, mark), f32),
        pltpu.VMEM((3, py, own, mark), f32),
        pltpu.VMEM((3, px, py * 2, mark), f32),
        pltpu.VMEM((3, px, py * 2, mark), f32),
        pltpu.VMEM((slots, size_z, kern * mark), bf16),
        pltpu.VMEM((3, size_x, size_y, size_z), f32),
        pltpu.VMEM((19, size_x, size_y, size_z), f32),
        pltpu.VMEM((2, 5, size_y, size_z), f32),
        pltpu.VMEM((2, 5, size_y, size_z), f32),
        pltpu.VMEM((2, face_rows, size_z), f32),
        pltpu.VMEM((2, 3, face_rows, size_z), f32),
        pltpu.VMEM((2, size_y, size_z), f32),
        pltpu.VMEM((2, 5, size_y, size_z), f32),
        pltpu.SemaphoreType.DMA((13,)),
        pltpu.SemaphoreType.DMA((13,)),
        pltpu.SemaphoreType.DMA((18,)),
        pltpu.SemaphoreType.DMA((18,)),
    ]
    populations_next, marker_force = pl.pallas_call(
        functools.partial(kernel, px, py, pz),
        out_shape=(
            jax.ShapeDtypeStruct(populations.shape, f32),
            jax.ShapeDtypeStruct((own, 3, mark), f32),
        ),
        in_specs=[vmem] * 8 + [smem],
        out_specs=(vmem, vmem),
        scratch_shapes=scratch,
        compiler_params=pltpu.CompilerParams(
            collective_id=0, has_side_effects=True, vmem_limit_bytes=48 << 20
        ),
        name="step",
    )(
        populations,
        solid_cells,
        slot_cells.reshape(slots, kern, mark),
        slot_weights.reshape(slots, kern, mark),
        slot_owner.reshape(1, slots),
        slot_block.reshape(1, slots),
        train_of_block.reshape(1, own),
        marker_area.reshape(own, mark),
        train_velocity,
    )
    return (populations_next, marker_force.reshape(1, 1, 1, own, 3, mark))


def solution(mesh):
    placed = (
        P(None, "gx", "gy", "gz"),
        P("gx", "gy", "gz"),
        P("gx", "gy", "gz", None, None, None),
        P("gx", "gy", "gz", None, None, None),
        P("gx", "gy", "gz", None, None),
        P("gx", "gy", "gz", None),
        P("gx", "gy", "gz", None),
        P("gx", "gy", "gz", None, None),
        P(),
    )
    return jax.shard_map(
        per_device,
        mesh=mesh,
        in_specs=placed,
        out_specs=(P(None, "gx", "gy", "gz"), P("gx", "gy", "gz", None, None, None)),
        check_vma=False,
    )
```

```python
import functools

import jax
import jax.numpy as jnp
import numpy as np
from jax import lax
from jax.experimental import pallas as pl
from jax.experimental.pallas import tpu as pltpu
from jax.sharding import PartitionSpec as P

velocity_table = np.array(
    [
        [0, 0, 0],
        [1, 0, 0],
        [-1, 0, 0],
        [0, 1, 0],
        [0, -1, 0],
        [0, 0, 1],
        [0, 0, -1],
        [1, 1, 0],
        [-1, -1, 0],
        [1, -1, 0],
        [-1, 1, 0],
        [1, 0, 1],
        [-1, 0, -1],
        [1, 0, -1],
        [-1, 0, 1],
        [0, 1, 1],
        [0, -1, -1],
        [0, 1, -1],
        [0, -1, 1],
    ]
)
weight_table = [1.0 / 3.0] + [1.0 / 18.0] * 6 + [1.0 / 36.0] * 12
opposite_table = [0, 2, 1, 4, 3, 6, 5, 8, 7, 10, 9, 12, 11, 14, 13, 16, 15, 18, 17]
stress_pairs = [(0, 0), (1, 1), (2, 2), (0, 1), (0, 2), (1, 2)]
tau_base = 0.55
smag_term = 18.0 * 1.4142135623730951 * 0.17 * 0.17
regular_eps = 0.0001
stiffness = 2.0
far_velocity = (0.02, 0.06, 0.0)
MESH = pl.DeviceIdType.MESH
f32 = jnp.float32
bf16 = jnp.bfloat16
i32 = jnp.int32

facing = [
    {sign: [q for q in range(19) if velocity_table[q][axis] == sign] for sign in (1, -1)}
    for axis in range(3)
]
Z_SIDES = ((0, 0), (1, 0), (-1, 0), (0, 1), (0, -1))
Y_SIDES = (0, 1, -1)


def project(direction, vector):
    projection = None
    for component in range(3):
        lattice_step = int(velocity_table[direction][component])
        if lattice_step != 0:
            term = vector[component] if lattice_step == 1 else -vector[component]
            projection = term if projection is None else projection + term
    return projection


def moments(populations):
    density = populations[0]
    momentum = [None, None, None]
    for direction in range(1, 19):
        density = density + populations[direction]
        for component in range(3):
            lattice_step = int(velocity_table[direction][component])
            if lattice_step != 0:
                term = populations[direction] if lattice_step == 1 else -populations[direction]
                momentum[component] = (
                    term if momentum[component] is None else momentum[component] + term
                )
    return (density, momentum)


def equilibrium(density, velocity):
    speed_sq = velocity[0] * velocity[0] + velocity[1] * velocity[1] + velocity[2] * velocity[2]
    base = 1.0 - 1.5 * speed_sq
    result = []
    for direction in range(19):
        projected = project(direction, velocity)
        inner = base if projected is None else base + projected * (3.0 + 4.5 * projected)
        result.append(weight_table[direction] * density * inner)
    return result


def far_field():
    speed_sq = sum(v * v for v in far_velocity)
    values = []
    for direction in range(19):
        projected = sum(int(velocity_table[direction][i]) * far_velocity[i] for i in range(3))
        values.append(
            weight_table[direction]
            * (1.0 + 3.0 * projected + 4.5 * projected * projected - 1.5 * speed_sq)
        )
    return values


def collide(populations, cell_force, solid):
    density, momentum = moments(populations)
    inverse = 1.0 / density
    velocity = [
        (momentum[component] + 0.5 * cell_force[component]) * inverse for component in range(3)
    ]
    balance = equilibrium(density, velocity)
    stress = [None] * 6
    departure = []
    for direction in range(19):
        non_eq = populations[direction] - balance[direction]
        departure.append(non_eq)
        for pair_pos in range(6):
            row_axis, col_axis = stress_pairs[pair_pos]
            factor = int(velocity_table[direction][row_axis] * velocity_table[direction][col_axis])
            if factor != 0:
                term = non_eq if factor == 1 else -non_eq
                stress[pair_pos] = term if stress[pair_pos] is None else stress[pair_pos] + term
    shear_sq = stress[0] * stress[0] + stress[1] * stress[1] + stress[2] * stress[2]
    shear_sq = shear_sq + 2.0 * (
        stress[3] * stress[3] + stress[4] * stress[4] + stress[5] * stress[5]
    )
    magnitude = jnp.sqrt(shear_sq + regular_eps)
    relax_time = 0.5 * (tau_base + jnp.sqrt(tau_base * tau_base + smag_term * magnitude * inverse))
    rate = 1.0 / relax_time
    guo_factor = 1.0 - 0.5 * rate
    speed_force = (
        velocity[0] * cell_force[0] + velocity[1] * cell_force[1] + velocity[2] * cell_force[2]
    )
    base = -3.0 * speed_force
    result = []
    for direction in range(19):
        along_force = project(direction, cell_force)
        along_speed = project(direction, velocity)
        inner = base if along_force is None else base + along_force * (3.0 + 9.0 * along_speed)
        relaxed = (
            populations[direction]
            - departure[direction] * rate
            + (guo_factor * weight_table[direction]) * inner
        )
        result.append(jnp.where(solid, populations[opposite_table[direction]], relaxed))
    return result


def pick_rows(one_hot, values):
    high = values.astype(bf16)
    rest = values - high.astype(f32)
    middle = rest.astype(bf16)
    low = (rest - middle.astype(f32)).astype(bf16)
    total = jnp.dot(one_hot, low, preferred_element_type=f32)
    total = total + jnp.dot(one_hot, middle, preferred_element_type=f32)
    return total + jnp.dot(one_hot, high, preferred_element_type=f32)


def iota(shape, dim):
    return lax.broadcasted_iota(i32, shape, dim)


def hot(condition):
    return jnp.where(condition, 1.0, 0.0).astype(bf16)


def to_column(row):
    n = row.shape[1]
    square = jnp.broadcast_to(row, (n, n))
    return jnp.sum(jnp.where(iota((n, n), 0) == iota((n, n), 1), square, 0.0), axis=1, keepdims=True)


def kernel(
    px,
    py,
    pz,
    pop_in,
    solid_in,
    cells_in,
    weights_in,
    owner_in,
    block_in,
    train_in,
    area_in,
    speed_in,
    out,
    force_out,
    pop,
    solid,
    cells,
    weights,
    owner,
    block,
    train,
    area,
    speed,
    table,
    rows,
    place,
    place_t,
    combine,
    combine_t,
    lab_send,
    lab_recv,
    z_send,
    z_recv,
    d_send,
    d_recv,
    f_all,
    r_send,
    r_recv,
    point_hot,
    cell_force,
    relaxed,
    x_send,
    x_recv,
    y_send,
    y_recv,
    t_send,
    t_recv,
    send_sem,
    recv_sem,
    halo_send,
    halo_recv,
    load_sem,
):
    slots, kern, mark = cells.shape
    size_x, size_y, size_z = pop.shape[1:]
    own = area.shape[0]
    cap = 2
    per_plane = py * cap
    total_rows = px * per_plane
    row_count = size_x * size_y
    gx, gy, gz = lax.axis_index("gx"), lax.axis_index("gy"), lax.axis_index("gz")

    def at(dx, dy, dz):
        return (
            lax.rem(gx + px + dx, px),
            lax.rem(gy + py + dy, py),
            lax.rem(gz + pz + dz, pz),
        )

    halo_far = (
        [(0, 0, s) for s in (1, -1)]
        + [(a, b, 0) for a in (1, -1) for b in (1, -1)]
        + [(a, 0, b) for a in (1, -1) for b in (1, -1)]
        + [(0, a, b) for a in (1, -1) for b in (1, -1)]
    )
    loads = [
        pltpu.make_async_copy(source, target, load_sem.at[n])
        for n, (source, target) in enumerate(
            (
                (owner_in, owner),
                (block_in, block),
                (pop_in, pop),
                (cells_in, cells),
                (weights_in, weights),
                (train_in, train),
                (area_in, area),
                (speed_in, speed),
                (solid_in, solid),
            )
        )
    ]
    for load in loads:
        load.start()
    barrier = pltpu.get_barrier_semaphore()

    def greet_x(k, _):
        pl.semaphore_signal(barrier, inc=1, device_id=at(k, 0, 0), device_id_type=MESH)
        return 0

    def greet_y(k, _):
        pl.semaphore_signal(barrier, inc=1, device_id=at(0, k, 0), device_id_type=MESH)
        return 0

    lax.fori_loop(1, px, greet_x, 0)
    lax.fori_loop(1, py, greet_y, 0)
    for place_of in halo_far:
        pl.semaphore_signal(barrier, inc=1, device_id=at(*place_of), device_id_type=MESH)

    loads[0].wait()
    loads[1].wait()
    owner_row = owner[...].astype(f32)
    owner_col = to_column(owner_row)
    same = owner_col == owner_row
    first, second = iota((slots, slots), 0), iota((slots, slots), 1)
    rank_row = jnp.sum(jnp.where(same & (first < second), 1.0, 0.0), axis=0, keepdims=True)
    rank_col = jnp.sum(jnp.where(same & (second < first), 1.0, 0.0), axis=1, keepdims=True)
    target_row = (owner_row * cap + rank_row).astype(i32)
    target_col = (owner_col * cap + rank_col).astype(i32)
    place[...] = hot(iota((total_rows, slots), 0) == target_row)
    place_t[...] = hot(iota((slots, total_rows), 1) == target_col)
    label_col = to_column(block[...].astype(f32)) + 1.0
    half = mark // per_plane
    plane_hot = hot(iota((px, slots), 0) == target_row // per_plane)
    spot = lax.rem(target_col, per_plane) + per_plane * lax.rem(gx, half)
    label_hot = jnp.where(iota((slots, mark), 1) == spot, label_col, 0.0).astype(bf16)
    labels = jnp.dot(plane_hot, label_hot, preferred_element_type=f32)
    lab_send[...] = jnp.broadcast_to(labels[:, None, :], lab_send.shape)
    lab_recv[gx] = lab_send[gx]

    loads[2].wait()
    density, momentum = moments([pop[q] for q in range(19)])
    for c in range(3):
        table[c] = (momentum[c] / density).reshape(row_count, size_z)


    def send_x(source, target, stage):
        def step(i, _):
            k = px // 2 + ((i + 1) // 2) * (1 - 2 * lax.rem(i, 2))
            peer = at(k, 0, 0)
            pltpu.make_async_remote_copy(
                src_ref=source.at[peer[0]],
                dst_ref=target.at[gx],
                send_sem=send_sem.at[stage],
                recv_sem=recv_sem.at[stage],
                device_id=peer,
                device_id_type=MESH,
            ).start()
            return 0

        lax.fori_loop(0, px - 1, step, 0)

    def send_y(source, own_place, target, stage):
        def step(k, _):
            peer = at(0, k, 0)
            pltpu.make_async_remote_copy(
                src_ref=source.at[gy if own_place else peer[1]],
                dst_ref=target.at[gy],
                send_sem=send_sem.at[stage],
                recv_sem=recv_sem.at[stage],
                device_id=peer,
                device_id_type=MESH,
            ).start()
            return 0

        lax.fori_loop(1, py, step, 0)

    def wait_for(buffer, count, semaphore):
        part = buffer.at[pl.ds(0, count)]
        pltpu.make_async_copy(part, part, semaphore).wait()

    LAB, ZS, DS, FS, RS = 0, 1, 4, 7, 10
    pl.semaphore_wait(barrier, px - 1 + py - 1 + len(halo_far))
    send_x(lab_send, lab_recv, LAB)

    def gather(c):
        def step(s, _):
            index = cells[s]
            lane = index & (size_z - 1)
            line = index // size_z
            found = jnp.zeros((kern, mark), f32)
            for h in range(row_count):
                entry = jnp.broadcast_to(table[c, h : h + 1, :], (kern, size_z))
                found = jnp.where(line == h, jnp.take_along_axis(entry, lane, axis=1), found)
            rows[c, pl.ds(s, 1), :] = jnp.sum(found * weights[s], axis=0, keepdims=True)
            return 0

        lax.fori_loop(0, slots, step, 0, unroll=8)

    def send_rows(c):
        z_send[c] = pick_rows(place[...], rows[c]).reshape(px, per_plane, mark)
        z_recv[c, gx] = z_send[c, gx]
        send_x(z_send.at[c], z_recv.at[c], ZS + c)

    def read_labels():
        wait_for(lab_recv, px - 1, recv_sem.at[LAB])
        parts, columns = [], []
        for n in range(total_rows // mark):
            label = jnp.sum(lab_recv[n * half : (n + 1) * half], axis=0)[0:1]
            group = lax.rem(iota((1, mark), 1), per_plane) // cap
            key = jnp.where(label > 0.5, group.astype(f32) * own + label - 1.0, -1.0)
            parts.append(key)
            columns.append(to_column(key))
        key_row = jnp.concatenate(parts, axis=1).astype(i32)
        key_col = jnp.concatenate(columns, axis=0).astype(i32)
        combine[...] = hot(iota((py * own, total_rows), 0) == key_row)
        combine_t[...] = hot(iota((total_rows, py * own), 1) == key_col)

    def send_sums(c):
        wait_for(z_recv.at[c], px - 1, recv_sem.at[ZS + c])
        d_send[c] = pick_rows(combine[...], z_recv[c].reshape(total_rows, mark)).reshape(
            py, own, mark
        )
        d_recv[c, gy] = d_send[c, gy]
        send_y(d_send.at[c], False, d_recv.at[c], DS + c)

    for load in loads[5:]:
        load.wait()
    train_col = to_column(train[...].astype(f32))

    def send_force(c):
        wait_for(d_recv.at[c], py - 1, recv_sem.at[DS + c])
        marker_velocity = d_recv[c, 0]
        for n in range(1, py):
            marker_velocity = marker_velocity + d_recv[c, n]
        goal = jnp.zeros((own, 1), f32)
        for t in range(speed.shape[0]):
            goal = jnp.where(train_col == float(t), speed[t, c], goal)
        force = stiffness * area[...] * (goal - marker_velocity)
        force_out[c] = force
        f_all[c, gy] = force
        send_y(f_all.at[c], True, f_all.at[c], FS + c)

    def send_back(c):
        wait_for(f_all.at[c], py - 1, recv_sem.at[FS + c])
        r_send[c] = pick_rows(combine_t[...], f_all[c].reshape(py * own, mark)).reshape(
            px, per_plane, mark
        )
        r_recv[c, gx] = r_send[c, gx]
        send_x(r_send.at[c], r_recv.at[c], RS + c)

    def point_one_hots(begin, end):
        def step(s, _):
            lane = (cells[s] & (size_z - 1)).astype(f32)
            columns = jnp.transpose(jnp.concatenate([lane] * (mark // kern), axis=0))
            place_of = iota((mark, size_z), 1).astype(f32).astype(bf16)
            for k in range(kern):
                wanted = jnp.broadcast_to(columns[:, k : k + 1], (mark, size_z)).astype(bf16)
                point_hot[s, k * mark : (k + 1) * mark, :] = jnp.where(
                    wanted == place_of, bf16(1), bf16(0)
                )
            return 0

        lax.fori_loop(begin, end, step, 0, unroll=4)

    def spread(c):
        wait_for(r_recv.at[c], px - 1, recv_sem.at[RS + c])
        rows[c] = pick_rows(place_t[...], r_recv[c].reshape(total_rows, mark))

        def step(s, total):
            line = (cells[s] // size_z).astype(f32)
            value = weights[s] * rows[c, pl.ds(s, 1), :]
            high = value.astype(bf16).astype(f32)
            low = value - high
            zero = bf16(0)
            columns = []
            for k in range(kern):
                wanted = jnp.broadcast_to(line[k : k + 1, :], (16, mark)).astype(bf16)
                pieces = []
                for piece in (high, low):
                    spread_piece = jnp.broadcast_to(piece[k : k + 1, :], (16, mark)).astype(bf16)
                    for j in range(row_count // 16):
                        place_of = (iota((16, mark), 0) + 16 * j).astype(f32).astype(bf16)
                        pieces.append(jnp.where(wanted == place_of, spread_piece, zero))
                columns.append(jnp.concatenate(pieces, axis=0))
            return total + jnp.dot(
                jnp.concatenate(columns, axis=1), point_hot[s], preferred_element_type=f32
            )

        total = lax.fori_loop(
            0, slots, step, jnp.zeros((2 * row_count, size_z), f32), unroll=8
        )
        cell_force[c] = (total[:row_count] + total[row_count:]).reshape(size_x, size_y, size_z)

    loads[3].wait()
    loads[4].wait()
    gather(0)
    send_rows(0)
    gather(1)
    send_rows(1)
    read_labels()
    gather(2)
    send_rows(2)
    send_sums(0)
    point_one_hots(0, slots // 4)
    send_force(0)
    point_one_hots(slots // 4, slots // 2)
    send_back(0)
    send_sums(1)
    point_one_hots(slots // 2, 3 * slots // 4)
    send_force(1)
    point_one_hots(3 * slots // 4, slots)
    send_back(1)
    send_sums(2)
    send_force(2)
    send_back(2)
    spread(0)
    spread(1)
    spread(2)

    def relax(x, _):
        result = collide(
            [pop[q, x] for q in range(19)], [cell_force[c, x] for c in range(3)], solid[x] == 1
        )
        for q in range(19):
            relaxed[q, x] = result[q]
        return 0

    lax.fori_loop(0, size_x, relax, 0)

    lane_at = iota((size_y, size_z), 1)
    line_at = iota((size_y, size_z), 0)
    halo = []

    def send_halo(source, target, place_of):
        n = len(halo)
        copy = pltpu.make_async_remote_copy(
            src_ref=source,
            dst_ref=target,
            send_sem=halo_send.at[n],
            recv_sem=halo_recv.at[n],
            device_id=at(*place_of),
            device_id_type=MESH,
        )
        copy.start()
        halo.append(copy)

    for d, sign in enumerate((1, -1)):
        tile = jnp.zeros((size_y, size_z), f32)
        edge = size_z - 1 if sign == 1 else 0
        for n, q in enumerate(facing[2][sign]):
            for x in range(size_x):
                column = jnp.broadcast_to(relaxed[q, x][:, edge : edge + 1], (size_y, size_z))
                tile = jnp.where(lane_at == n * size_x + x, column, tile)
        t_send[d] = tile
        for side, (dx, dy) in enumerate(Z_SIDES):
            send_halo(t_send.at[d], t_recv.at[d, side], (dx, dy, sign))
    for d, sign in enumerate((1, -1)):
        edge = size_y - 1 if sign == 1 else 0
        for n, q in enumerate(facing[1][sign]):
            y_send[d, n * size_x : (n + 1) * size_x, :] = relaxed[q, :, edge, :]
        for side, dx in enumerate(Y_SIDES):
            send_halo(y_send.at[d], y_recv.at[d, side], (dx, sign, 0))
    for d, sign in enumerate((1, -1)):
        edge = size_x - 1 if sign == 1 else 0
        for n, q in enumerate(facing[0][sign]):
            x_send[d, n] = relaxed[q, edge]
        send_halo(x_send.at[d], x_recv.at[d], (sign, 0, 0))
    for copy in halo:
        copy.wait_recv()

    on_side = (
        ((line_at == 0) & (gy == 0))
        | ((line_at == size_y - 1) & (gy == py - 1))
        | ((lane_at == 0) & (gz == 0))
        | ((lane_at == size_z - 1) & (gz == pz - 1))
    )
    far = far_field()
    for q in range(19):
        cx, cy, cz = (int(v) for v in velocity_table[q])
        for x in range(size_x):
            source = x - cx
            inside = 0 <= source < size_x
            at_edge = source % size_x
            if inside:
                plane = relaxed[q, source]
            else:
                plane = x_recv[0 if cx == 1 else 1, facing[0][cx].index(q)]
            side = 0 if inside else (1 if cx == 1 else 2)
            if cy != 0:
                d = 0 if cy == 1 else 1
                n = facing[1][cy].index(q) * size_x + at_edge
                row = jnp.broadcast_to(y_recv[d, side, n : n + 1, :], (size_y, size_z))
                plane = pltpu.roll(plane, cy % size_y, 0)
                plane = jnp.where(line_at == (0 if cy == 1 else size_y - 1), row, plane)
            if cz != 0:
                d = 0 if cz == 1 else 1
                n = facing[2][cz].index(q) * size_x + at_edge
                tile = t_recv[d, side]
                if cy != 0:
                    beside = pltpu.roll(t_recv[d, 3 if cy == 1 else 4], cy % size_y, 0)
                    tile = pltpu.roll(tile, cy % size_y, 0)
                    tile = jnp.where(line_at == (0 if cy == 1 else size_y - 1), beside, tile)
                column = jnp.broadcast_to(tile[:, n : n + 1], (size_y, size_z))
                plane = pltpu.roll(plane, cz % size_z, 1)
                plane = jnp.where(lane_at == (0 if cz == 1 else size_z - 1), column, plane)
            out[q, x] = jnp.where(on_side, f32(far[q]), plane)

    wait_for(lab_send, px - 1, send_sem.at[LAB])
    for c in range(3):
        wait_for(z_send.at[c], px - 1, send_sem.at[ZS + c])
        wait_for(d_send.at[c], py - 1, send_sem.at[DS + c])
        wait_for(f_all.at[c], py - 1, send_sem.at[FS + c])
        wait_for(r_send.at[c], px - 1, send_sem.at[RS + c])
    for copy in halo:
        copy.wait_send()


def per_device(
    populations,
    solid_cells,
    slot_cells,
    slot_weights,
    slot_owner,
    slot_block,
    train_of_block,
    marker_area,
    train_velocity,
):
    px, py, pz = (lax.axis_size(axis) for axis in ("gx", "gy", "gz"))
    slots, kern, mark = slot_cells.shape[3:]
    own = train_of_block.shape[3]
    _, size_x, size_y, size_z = populations.shape
    rows_out = px * py * 2
    vmem = pl.BlockSpec(memory_space=pltpu.VMEM)
    hbm = pl.BlockSpec(memory_space=pltpu.HBM)
    face = 5 * size_x
    face_rows = -(-face // 8) * 8
    scratch = [
        pltpu.VMEM(populations.shape, f32),
        pltpu.VMEM(solid_cells.shape, i32),
        pltpu.VMEM((slots, kern, mark), i32),
        pltpu.VMEM((slots, kern, mark), f32),
        pltpu.VMEM((1, slots), i32),
        pltpu.VMEM((1, slots), i32),
        pltpu.VMEM((1, own), i32),
        pltpu.VMEM((own, mark), f32),
        pltpu.SMEM(train_velocity.shape, f32),
        pltpu.VMEM((3, size_x * size_y, size_z), f32),
        pltpu.VMEM((3, slots, mark), f32),
        pltpu.VMEM((rows_out, slots), bf16),
        pltpu.VMEM((slots, rows_out), bf16),
        pltpu.VMEM((py * own, rows_out), bf16),
        pltpu.VMEM((rows_out, py * own), bf16),
        pltpu.VMEM((px, 8, mark), f32),
        pltpu.VMEM((px, 8, mark), f32),
        pltpu.VMEM((3, px, py * 2, mark), f32),
        pltpu.VMEM((3, px, py * 2, mark), f32),
        pltpu.VMEM((3, py, own, mark), f32),
        pltpu.VMEM((3, py, own, mark), f32),
        pltpu.VMEM((3, py, own, mark), f32),
        pltpu.VMEM((3, px, py * 2, mark), f32),
        pltpu.VMEM((3, px, py * 2, mark), f32),
        pltpu.VMEM((slots, kern * mark, size_z), bf16),
        pltpu.VMEM((3, size_x, size_y, size_z), f32),
        pltpu.VMEM((19, size_x, size_y, size_z), f32),
        pltpu.VMEM((2, 5, size_y, size_z), f32),
        pltpu.VMEM((2, 5, size_y, size_z), f32),
        pltpu.VMEM((2, face_rows, size_z), f32),
        pltpu.VMEM((2, 3, face_rows, size_z), f32),
        pltpu.VMEM((2, size_y, size_z), f32),
        pltpu.VMEM((2, 5, size_y, size_z), f32),
        pltpu.SemaphoreType.DMA((13,)),
        pltpu.SemaphoreType.DMA((13,)),
        pltpu.SemaphoreType.DMA((18,)),
        pltpu.SemaphoreType.DMA((18,)),
        pltpu.SemaphoreType.DMA((9,)),
    ]
    populations_next, marker_force = pl.pallas_call(
        functools.partial(kernel, px, py, pz),
        out_shape=(
            jax.ShapeDtypeStruct(populations.shape, f32),
            jax.ShapeDtypeStruct((3, own, mark), f32),
        ),
        in_specs=[hbm] * 9,
        out_specs=(vmem, vmem),
        scratch_shapes=scratch,
        compiler_params=pltpu.CompilerParams(
            collective_id=0, has_side_effects=True, vmem_limit_bytes=60 << 20
        ),
        name="step",
    )(
        populations,
        solid_cells,
        slot_cells.reshape(slots, kern, mark),
        slot_weights.reshape(slots, kern, mark),
        slot_owner.reshape(1, slots),
        slot_block.reshape(1, slots),
        train_of_block.reshape(1, own),
        marker_area.reshape(own, mark),
        train_velocity,
    )
    return (populations_next, marker_force.transpose(1, 0, 2).reshape(1, 1, 1, own, 3, mark))


def solution(mesh):
    placed = (
        P(None, "gx", "gy", "gz"),
        P("gx", "gy", "gz"),
        P("gx", "gy", "gz", None, None, None),
        P("gx", "gy", "gz", None, None, None),
        P("gx", "gy", "gz", None, None),
        P("gx", "gy", "gz", None),
        P("gx", "gy", "gz", None),
        P("gx", "gy", "gz", None, None),
        P(),
    )
    return jax.shard_map(
        per_device,
        mesh=mesh,
        in_specs=placed,
        out_specs=(P(None, "gx", "gy", "gz"), P("gx", "gy", "gz", None, None, None)),
        check_vma=False,
    )
```

```python
import functools

import jax
import jax.numpy as jnp
import numpy as np
from jax import lax
from jax.experimental import pallas as pl
from jax.experimental.pallas import tpu as pltpu
from jax.sharding import PartitionSpec as P

velocity_table = np.array(
    [
        [0, 0, 0],
        [1, 0, 0],
        [-1, 0, 0],
        [0, 1, 0],
        [0, -1, 0],
        [0, 0, 1],
        [0, 0, -1],
        [1, 1, 0],
        [-1, -1, 0],
        [1, -1, 0],
        [-1, 1, 0],
        [1, 0, 1],
        [-1, 0, -1],
        [1, 0, -1],
        [-1, 0, 1],
        [0, 1, 1],
        [0, -1, -1],
        [0, 1, -1],
        [0, -1, 1],
    ]
)
weight_table = [1.0 / 3.0] + [1.0 / 18.0] * 6 + [1.0 / 36.0] * 12
opposite_table = [0, 2, 1, 4, 3, 6, 5, 8, 7, 10, 9, 12, 11, 14, 13, 16, 15, 18, 17]
stress_pairs = [(0, 0), (1, 1), (2, 2), (0, 1), (0, 2), (1, 2)]
tau_base = 0.55
smag_term = 18.0 * 1.4142135623730951 * 0.17 * 0.17
regular_eps = 0.0001
stiffness = 2.0
far_velocity = (0.02, 0.06, 0.0)
MESH = pl.DeviceIdType.MESH
f32 = jnp.float32
bf16 = jnp.bfloat16
i32 = jnp.int32

facing = [
    {sign: [q for q in range(19) if velocity_table[q][axis] == sign] for sign in (1, -1)}
    for axis in range(3)
]
Z_SIDES = ((0, 0), (1, 0), (-1, 0), (0, 1), (0, -1))
Y_SIDES = (0, 1, -1)


def project(direction, vector):
    projection = None
    for component in range(3):
        lattice_step = int(velocity_table[direction][component])
        if lattice_step != 0:
            term = vector[component] if lattice_step == 1 else -vector[component]
            projection = term if projection is None else projection + term
    return projection


def moments(populations):
    density = populations[0]
    momentum = [None, None, None]
    for direction in range(1, 19):
        density = density + populations[direction]
        for component in range(3):
            lattice_step = int(velocity_table[direction][component])
            if lattice_step != 0:
                term = populations[direction] if lattice_step == 1 else -populations[direction]
                momentum[component] = (
                    term if momentum[component] is None else momentum[component] + term
                )
    return (density, momentum)


def equilibrium(density, velocity):
    speed_sq = velocity[0] * velocity[0] + velocity[1] * velocity[1] + velocity[2] * velocity[2]
    base = 1.0 - 1.5 * speed_sq
    result = []
    for direction in range(19):
        projected = project(direction, velocity)
        inner = base if projected is None else base + projected * (3.0 + 4.5 * projected)
        result.append(weight_table[direction] * density * inner)
    return result


def far_field():
    speed_sq = sum(v * v for v in far_velocity)
    values = []
    for direction in range(19):
        projected = sum(int(velocity_table[direction][i]) * far_velocity[i] for i in range(3))
        values.append(
            weight_table[direction]
            * (1.0 + 3.0 * projected + 4.5 * projected * projected - 1.5 * speed_sq)
        )
    return values


def collide(populations, cell_force, solid):
    density, momentum = moments(populations)
    inverse = 1.0 / density
    velocity = [
        (momentum[component] + 0.5 * cell_force[component]) * inverse for component in range(3)
    ]
    balance = equilibrium(density, velocity)
    stress = [None] * 6
    departure = []
    for direction in range(19):
        non_eq = populations[direction] - balance[direction]
        departure.append(non_eq)
        for pair_pos in range(6):
            row_axis, col_axis = stress_pairs[pair_pos]
            factor = int(velocity_table[direction][row_axis] * velocity_table[direction][col_axis])
            if factor != 0:
                term = non_eq if factor == 1 else -non_eq
                stress[pair_pos] = term if stress[pair_pos] is None else stress[pair_pos] + term
    shear_sq = stress[0] * stress[0] + stress[1] * stress[1] + stress[2] * stress[2]
    shear_sq = shear_sq + 2.0 * (
        stress[3] * stress[3] + stress[4] * stress[4] + stress[5] * stress[5]
    )
    magnitude = jnp.sqrt(shear_sq + regular_eps)
    relax_time = 0.5 * (tau_base + jnp.sqrt(tau_base * tau_base + smag_term * magnitude * inverse))
    rate = 1.0 / relax_time
    guo_factor = 1.0 - 0.5 * rate
    speed_force = (
        velocity[0] * cell_force[0] + velocity[1] * cell_force[1] + velocity[2] * cell_force[2]
    )
    base = -3.0 * speed_force
    result = []
    for direction in range(19):
        along_force = project(direction, cell_force)
        along_speed = project(direction, velocity)
        inner = base if along_force is None else base + along_force * (3.0 + 9.0 * along_speed)
        relaxed = (
            populations[direction]
            - departure[direction] * rate
            + (guo_factor * weight_table[direction]) * inner
        )
        result.append(jnp.where(solid, populations[opposite_table[direction]], relaxed))
    return result


def pick_rows(one_hot, values):
    high = values.astype(bf16)
    rest = values - high.astype(f32)
    middle = rest.astype(bf16)
    low = (rest - middle.astype(f32)).astype(bf16)
    total = jnp.dot(one_hot, low, preferred_element_type=f32)
    total = total + jnp.dot(one_hot, middle, preferred_element_type=f32)
    return total + jnp.dot(one_hot, high, preferred_element_type=f32)


def iota(shape, dim):
    return lax.broadcasted_iota(i32, shape, dim)


def hot(condition):
    return jnp.where(condition, 1.0, 0.0).astype(bf16)


def to_column(row):
    n = row.shape[1]
    square = jnp.broadcast_to(row, (n, n))
    return jnp.sum(jnp.where(iota((n, n), 0) == iota((n, n), 1), square, 0.0), axis=1, keepdims=True)


def kernel(
    px,
    py,
    pz,
    pop_in,
    solid_in,
    cells_in,
    weights_in,
    owner_in,
    block_in,
    train_in,
    area_in,
    speed_in,
    out,
    force_out,
    pop,
    solid,
    cells,
    weights,
    owner,
    block,
    train,
    area,
    speed,
    table,
    rows,
    place,
    place_t,
    combine,
    combine_t,
    lab_send,
    lab_recv,
    z_send,
    z_recv,
    d_send,
    d_recv,
    f_all,
    r_send,
    r_recv,
    point_hot,
    cell_force,
    relaxed,
    x_send,
    x_recv,
    y_send,
    y_recv,
    t_send,
    t_recv,
    send_sem,
    recv_sem,
    halo_send,
    halo_recv,
    load_sem,
):
    slots, kern, mark = cells.shape
    size_x, size_y, size_z = pop.shape[1:]
    own = area.shape[0]
    cap = 2
    per_plane = py * cap
    total_rows = px * per_plane
    row_count = size_x * size_y
    gx, gy, gz = lax.axis_index("gx"), lax.axis_index("gy"), lax.axis_index("gz")

    def at(dx, dy, dz):
        return (
            lax.rem(gx + px + dx, px),
            lax.rem(gy + py + dy, py),
            lax.rem(gz + pz + dz, pz),
        )

    halo_far = (
        [(0, 0, s) for s in (1, -1)]
        + [(a, b, 0) for a in (1, -1) for b in (1, -1)]
        + [(a, 0, b) for a in (1, -1) for b in (1, -1)]
        + [(0, a, b) for a in (1, -1) for b in (1, -1)]
    )
    loads = [
        pltpu.make_async_copy(source, target, load_sem.at[n])
        for n, (source, target) in enumerate(
            (
                (owner_in, owner),
                (block_in, block),
                (pop_in, pop),
                (cells_in, cells),
                (weights_in, weights),
                (train_in, train),
                (area_in, area),
                (speed_in, speed),
                (solid_in, solid),
            )
        )
    ]
    for load in loads:
        load.start()
    barrier = pltpu.get_barrier_semaphore()

    def greet_x(k, _):
        pl.semaphore_signal(barrier, inc=1, device_id=at(k, 0, 0), device_id_type=MESH)
        return 0

    def greet_y(k, _):
        pl.semaphore_signal(barrier, inc=1, device_id=at(0, k, 0), device_id_type=MESH)
        return 0

    lax.fori_loop(1, px, greet_x, 0)
    lax.fori_loop(1, py, greet_y, 0)
    for place_of in halo_far:
        pl.semaphore_signal(barrier, inc=1, device_id=at(*place_of), device_id_type=MESH)

    loads[0].wait()
    loads[1].wait()
    owner_row = owner[...].astype(f32)
    owner_col = to_column(owner_row)
    same = owner_col == owner_row
    first, second = iota((slots, slots), 0), iota((slots, slots), 1)
    rank_row = jnp.sum(jnp.where(same & (first < second), 1.0, 0.0), axis=0, keepdims=True)
    rank_col = jnp.sum(jnp.where(same & (second < first), 1.0, 0.0), axis=1, keepdims=True)
    target_row = (owner_row * cap + rank_row).astype(i32)
    target_col = (owner_col * cap + rank_col).astype(i32)
    place[...] = hot(iota((total_rows, slots), 0) == target_row)
    place_t[...] = hot(iota((slots, total_rows), 1) == target_col)
    label_col = to_column(block[...].astype(f32)) + 1.0
    half = mark // per_plane
    plane_hot = hot(iota((px, slots), 0) == target_row // per_plane)
    spot = lax.rem(target_col, per_plane) + per_plane * lax.rem(gx, half)
    label_hot = jnp.where(iota((slots, mark), 1) == spot, label_col, 0.0).astype(bf16)
    labels = jnp.dot(plane_hot, label_hot, preferred_element_type=f32)
    for n in range(px):
        lab_send[n] = labels[n : n + 1]
    lab_recv[gx] = lab_send[gx]

    loads[2].wait()
    density, momentum = moments([pop[q] for q in range(19)])
    for c in range(3):
        table[c] = (momentum[c] / density).reshape(row_count, size_z)


    def send_x(source, target, stage):
        def step(i, _):
            k = px // 2 + ((i + 1) // 2) * (1 - 2 * lax.rem(i, 2))
            peer = at(k, 0, 0)
            pltpu.make_async_remote_copy(
                src_ref=source.at[peer[0]],
                dst_ref=target.at[gx],
                send_sem=send_sem.at[stage],
                recv_sem=recv_sem.at[stage],
                device_id=peer,
                device_id_type=MESH,
            ).start()
            return 0

        lax.fori_loop(0, px - 1, step, 0)

    def send_y(source, own_place, target, stage):
        def step(i, _):
            k = py // 2 + ((i + 1) // 2) * (1 - 2 * lax.rem(i, 2))
            peer = at(0, k, 0)
            pltpu.make_async_remote_copy(
                src_ref=source.at[gy if own_place else peer[1]],
                dst_ref=target.at[gy],
                send_sem=send_sem.at[stage],
                recv_sem=recv_sem.at[stage],
                device_id=peer,
                device_id_type=MESH,
            ).start()
            return 0

        lax.fori_loop(0, py - 1, step, 0)

    def wait_for(buffer, count, semaphore):
        part = buffer.at[pl.ds(0, count)]
        pltpu.make_async_copy(part, part, semaphore).wait()

    LAB, ZS, DS, FS, RS = 0, 1, 4, 7, 10

    def gather(c):
        def step(s, _):
            index = cells[s]
            lane = index & (size_z - 1)
            line = index // size_z
            found = jnp.zeros((kern, mark), f32)
            for h in range(row_count):
                entry = jnp.broadcast_to(table[c, h : h + 1, :], (kern, size_z))
                found = jnp.where(line == h, jnp.take_along_axis(entry, lane, axis=1), found)
            rows[c, pl.ds(s, 1), :] = jnp.sum(found * weights[s], axis=0, keepdims=True)
            return 0

        lax.fori_loop(0, slots, step, 0, unroll=8)

    def send_rows(c):
        z_send[c] = pick_rows(place[...], rows[c]).reshape(px, per_plane, mark)
        z_recv[c, gx] = z_send[c, gx]
        send_x(z_send.at[c], z_recv.at[c], ZS + c)

    def read_labels():
        wait_for(lab_recv, px - 1, recv_sem.at[LAB])
        parts, columns = [], []
        for n in range(total_rows // mark):
            label = jnp.sum(lab_recv[n * half : (n + 1) * half], axis=0)
            group = lax.rem(iota((1, mark), 1), per_plane) // cap
            key = jnp.where(label > 0.5, group.astype(f32) * own + label - 1.0, -1.0)
            parts.append(key)
            columns.append(to_column(key))
        key_row = jnp.concatenate(parts, axis=1).astype(i32)
        key_col = jnp.concatenate(columns, axis=0).astype(i32)
        combine[...] = hot(iota((py * own, total_rows), 0) == key_row)
        combine_t[...] = hot(iota((total_rows, py * own), 1) == key_col)

    def send_sums(c):
        wait_for(z_recv.at[c], px - 1, recv_sem.at[ZS + c])
        d_send[c] = pick_rows(combine[...], z_recv[c].reshape(total_rows, mark)).reshape(
            py, own, mark
        )
        d_recv[c, gy] = d_send[c, gy]
        send_y(d_send.at[c], False, d_recv.at[c], DS + c)

    for load in loads[5:]:
        load.wait()
    train_col = to_column(train[...].astype(f32))

    def send_force(c):
        wait_for(d_recv.at[c], py - 1, recv_sem.at[DS + c])
        marker_velocity = d_recv[c, 0]
        for n in range(1, py):
            marker_velocity = marker_velocity + d_recv[c, n]
        goal = jnp.zeros((own, 1), f32)
        for t in range(speed.shape[0]):
            goal = jnp.where(train_col == float(t), speed[t, c], goal)
        force = stiffness * area[...] * (goal - marker_velocity)
        force_out[c] = force
        f_all[c, gy] = force
        send_y(f_all.at[c], True, f_all.at[c], FS + c)

    def send_back(c):
        wait_for(f_all.at[c], py - 1, recv_sem.at[FS + c])
        r_send[c] = pick_rows(combine_t[...], f_all[c].reshape(py * own, mark)).reshape(
            px, per_plane, mark
        )
        r_recv[c, gx] = r_send[c, gx]
        send_x(r_send.at[c], r_recv.at[c], RS + c)

    def point_one_hots(begin, end):
        def step(s, _):
            lane = (cells[s] & (size_z - 1)).astype(f32)
            columns = jnp.transpose(jnp.concatenate([lane] * (mark // kern), axis=0))
            place_of = iota((mark, size_z), 1).astype(f32).astype(bf16)
            for k in range(kern):
                wanted = jnp.broadcast_to(columns[:, k : k + 1], (mark, size_z)).astype(bf16)
                point_hot[s, k * mark : (k + 1) * mark, :] = jnp.where(
                    wanted == place_of, bf16(1), bf16(0)
                )
            return 0

        lax.fori_loop(begin, end, step, 0, unroll=4)

    def spread(c):
        wait_for(r_recv.at[c], px - 1, recv_sem.at[RS + c])
        rows[c] = pick_rows(place_t[...], r_recv[c].reshape(total_rows, mark))

        def step(s, total):
            line = (cells[s] // size_z).astype(f32)
            value = weights[s] * rows[c, pl.ds(s, 1), :]
            high = value.astype(bf16).astype(f32)
            low = value - high
            zero = bf16(0)
            columns = []
            for k in range(kern):
                wanted = jnp.broadcast_to(line[k : k + 1, :], (16, mark)).astype(bf16)
                pieces = []
                for piece in (high, low):
                    spread_piece = jnp.broadcast_to(piece[k : k + 1, :], (16, mark)).astype(bf16)
                    for j in range(row_count // 16):
                        place_of = (iota((16, mark), 0) + 16 * j).astype(f32).astype(bf16)
                        pieces.append(jnp.where(wanted == place_of, spread_piece, zero))
                columns.append(jnp.concatenate(pieces, axis=0))
            return total + jnp.dot(
                jnp.concatenate(columns, axis=1), point_hot[s], preferred_element_type=f32
            )

        total = lax.fori_loop(
            0, slots, step, jnp.zeros((2 * row_count, size_z), f32), unroll=16
        )
        cell_force[c] = (total[:row_count] + total[row_count:]).reshape(size_x, size_y, size_z)

    loads[3].wait()
    loads[4].wait()
    gather(0)
    pl.semaphore_wait(barrier, px - 1 + py - 1 + len(halo_far))
    send_x(lab_send, lab_recv, LAB)
    send_rows(0)
    gather(1)
    send_rows(1)
    read_labels()
    gather(2)
    send_rows(2)
    send_sums(0)
    point_one_hots(0, 16)
    send_force(0)
    point_one_hots(16, 32)
    send_sums(1)
    point_one_hots(32, 48)
    send_force(1)
    send_sums(2)
    send_back(0)
    send_back(1)
    point_one_hots(48, 64)
    send_force(2)
    send_back(2)
    spread(0)
    spread(1)
    spread(2)

    def relax(x):
        result = collide(
            [pop[q, x] for q in range(19)], [cell_force[c, x] for c in range(3)], solid[x] == 1
        )
        for q in range(19):
            relaxed[q, x] = result[q]

    lane_at = iota((size_y, size_z), 1)
    line_at = iota((size_y, size_z), 0)
    halo = []

    def send_halo(source, target, place_of):
        n = len(halo)
        copy = pltpu.make_async_remote_copy(
            src_ref=source,
            dst_ref=target,
            send_sem=halo_send.at[n],
            recv_sem=halo_recv.at[n],
            device_id=at(*place_of),
            device_id_type=MESH,
        )
        copy.start()
        halo.append(copy)

    relax(0)
    relax(size_x - 1)
    for d, sign in enumerate((1, -1)):
        edge = size_x - 1 if sign == 1 else 0
        for n, q in enumerate(facing[0][sign]):
            x_send[d, n] = relaxed[q, edge]
        send_halo(x_send.at[d], x_recv.at[d], (sign, 0, 0))
    for x in range(1, size_x - 1):
        relax(x)
    for d, sign in enumerate((1, -1)):
        tile = jnp.zeros((size_y, size_z), f32)
        edge = size_z - 1 if sign == 1 else 0
        for n, q in enumerate(facing[2][sign]):
            for x in range(size_x):
                column = jnp.broadcast_to(relaxed[q, x][:, edge : edge + 1], (size_y, size_z))
                tile = jnp.where(lane_at == n * size_x + x, column, tile)
        t_send[d] = tile
        for side, (dx, dy) in reversed(list(enumerate(Z_SIDES))):
            send_halo(t_send.at[d], t_recv.at[d, side], (dx, dy, sign))
    for d, sign in enumerate((1, -1)):
        edge = size_y - 1 if sign == 1 else 0
        for n, q in enumerate(facing[1][sign]):
            y_send[d, n * size_x : (n + 1) * size_x, :] = relaxed[q, :, edge, :]
        for side, dx in reversed(list(enumerate(Y_SIDES))):
            send_halo(y_send.at[d], y_recv.at[d, side], (dx, sign, 0))
    for copy in halo:
        copy.wait_recv()

    on_side = (
        ((line_at == 0) & (gy == 0))
        | ((line_at == size_y - 1) & (gy == py - 1))
        | ((lane_at == 0) & (gz == 0))
        | ((lane_at == size_z - 1) & (gz == pz - 1))
    )
    far = far_field()
    for q in range(19):
        cx, cy, cz = (int(v) for v in velocity_table[q])
        for x in range(size_x):
            source = x - cx
            inside = 0 <= source < size_x
            at_edge = source % size_x
            if inside:
                plane = relaxed[q, source]
            else:
                plane = x_recv[0 if cx == 1 else 1, facing[0][cx].index(q)]
            side = 0 if inside else (1 if cx == 1 else 2)
            if cy != 0:
                d = 0 if cy == 1 else 1
                n = facing[1][cy].index(q) * size_x + at_edge
                row = jnp.broadcast_to(y_recv[d, side, n : n + 1, :], (size_y, size_z))
                plane = pltpu.roll(plane, cy % size_y, 0)
                plane = jnp.where(line_at == (0 if cy == 1 else size_y - 1), row, plane)
            if cz != 0:
                d = 0 if cz == 1 else 1
                n = facing[2][cz].index(q) * size_x + at_edge
                tile = t_recv[d, side]
                if cy != 0:
                    beside = pltpu.roll(t_recv[d, 3 if cy == 1 else 4], cy % size_y, 0)
                    tile = pltpu.roll(tile, cy % size_y, 0)
                    tile = jnp.where(line_at == (0 if cy == 1 else size_y - 1), beside, tile)
                column = jnp.broadcast_to(tile[:, n : n + 1], (size_y, size_z))
                plane = pltpu.roll(plane, cz % size_z, 1)
                plane = jnp.where(lane_at == (0 if cz == 1 else size_z - 1), column, plane)
            out[q, x] = jnp.where(on_side, f32(far[q]), plane)

    wait_for(lab_send, px - 1, send_sem.at[LAB])
    for c in range(3):
        wait_for(z_send.at[c], px - 1, send_sem.at[ZS + c])
        wait_for(d_send.at[c], py - 1, send_sem.at[DS + c])
        wait_for(f_all.at[c], py - 1, send_sem.at[FS + c])
        wait_for(r_send.at[c], px - 1, send_sem.at[RS + c])
    for copy in halo:
        copy.wait_send()


def per_device(
    populations,
    solid_cells,
    slot_cells,
    slot_weights,
    slot_owner,
    slot_block,
    train_of_block,
    marker_area,
    train_velocity,
):
    px, py, pz = (lax.axis_size(axis) for axis in ("gx", "gy", "gz"))
    slots, kern, mark = slot_cells.shape[3:]
    own = train_of_block.shape[3]
    _, size_x, size_y, size_z = populations.shape
    rows_out = px * py * 2
    vmem = pl.BlockSpec(memory_space=pltpu.VMEM)
    hbm = pl.BlockSpec(memory_space=pltpu.HBM)
    face = 5 * size_x
    face_rows = -(-face // 8) * 8
    scratch = [
        pltpu.VMEM(populations.shape, f32),
        pltpu.VMEM(solid_cells.shape, i32),
        pltpu.VMEM((slots, kern, mark), i32),
        pltpu.VMEM((slots, kern, mark), f32),
        pltpu.VMEM((1, slots), i32),
        pltpu.VMEM((1, slots), i32),
        pltpu.VMEM((1, own), i32),
        pltpu.VMEM((own, mark), f32),
        pltpu.SMEM(train_velocity.shape, f32),
        pltpu.VMEM((3, size_x * size_y, size_z), f32),
        pltpu.VMEM((3, slots, mark), f32),
        pltpu.VMEM((rows_out, slots), bf16),
        pltpu.VMEM((slots, rows_out), bf16),
        pltpu.VMEM((py * own, rows_out), bf16),
        pltpu.VMEM((rows_out, py * own), bf16),
        pltpu.VMEM((px, 1, mark), f32),
        pltpu.VMEM((px, 1, mark), f32),
        pltpu.VMEM((3, px, py * 2, mark), f32),
        pltpu.VMEM((3, px, py * 2, mark), f32),
        pltpu.VMEM((3, py, own, mark), f32),
        pltpu.VMEM((3, py, own, mark), f32),
        pltpu.VMEM((3, py, own, mark), f32),
        pltpu.VMEM((3, px, py * 2, mark), f32),
        pltpu.VMEM((3, px, py * 2, mark), f32),
        pltpu.VMEM((slots, kern * mark, size_z), bf16),
        pltpu.VMEM((3, size_x, size_y, size_z), f32),
        pltpu.VMEM((19, size_x, size_y, size_z), f32),
        pltpu.VMEM((2, 5, size_y, size_z), f32),
        pltpu.VMEM((2, 5, size_y, size_z), f32),
        pltpu.VMEM((2, face_rows, size_z), f32),
        pltpu.VMEM((2, 3, face_rows, size_z), f32),
        pltpu.VMEM((2, size_y, size_z), f32),
        pltpu.VMEM((2, 5, size_y, size_z), f32),
        pltpu.SemaphoreType.DMA((13,)),
        pltpu.SemaphoreType.DMA((13,)),
        pltpu.SemaphoreType.DMA((18,)),
        pltpu.SemaphoreType.DMA((18,)),
        pltpu.SemaphoreType.DMA((9,)),
    ]
    populations_next, marker_force = pl.pallas_call(
        functools.partial(kernel, px, py, pz),
        out_shape=(
            pltpu.VMEM(populations.shape, f32),
            pltpu.VMEM((3, own, mark), f32),
        ),
        in_specs=[hbm] * 9,
        out_specs=(vmem, vmem),
        scratch_shapes=scratch,
        compiler_params=pltpu.CompilerParams(
            collective_id=0, has_side_effects=True, vmem_limit_bytes=60 << 20
        ),
        name="step",
    )(
        populations,
        solid_cells,
        slot_cells.reshape(slots, kern, mark),
        slot_weights.reshape(slots, kern, mark),
        slot_owner.reshape(1, slots),
        slot_block.reshape(1, slots),
        train_of_block.reshape(1, own),
        marker_area.reshape(own, mark),
        train_velocity,
    )
    return (populations_next, marker_force.transpose(1, 0, 2).reshape(1, 1, 1, own, 3, mark))


def solution(mesh):
    placed = (
        P(None, "gx", "gy", "gz"),
        P("gx", "gy", "gz"),
        P("gx", "gy", "gz", None, None, None),
        P("gx", "gy", "gz", None, None, None),
        P("gx", "gy", "gz", None, None),
        P("gx", "gy", "gz", None),
        P("gx", "gy", "gz", None),
        P("gx", "gy", "gz", None, None),
        P(),
    )
    return jax.shard_map(
        per_device,
        mesh=mesh,
        in_specs=placed,
        out_specs=(P(None, "gx", "gy", "gz"), P("gx", "gy", "gz", None, None, None)),
        check_vma=False,
    )
```

```python
import functools

import jax
import jax.numpy as jnp
import numpy as np
from jax import lax
from jax.experimental import pallas as pl
from jax.experimental.pallas import tpu as pltpu
from jax.sharding import PartitionSpec as P

velocity_table = np.array(
    [
        [0, 0, 0],
        [1, 0, 0],
        [-1, 0, 0],
        [0, 1, 0],
        [0, -1, 0],
        [0, 0, 1],
        [0, 0, -1],
        [1, 1, 0],
        [-1, -1, 0],
        [1, -1, 0],
        [-1, 1, 0],
        [1, 0, 1],
        [-1, 0, -1],
        [1, 0, -1],
        [-1, 0, 1],
        [0, 1, 1],
        [0, -1, -1],
        [0, 1, -1],
        [0, -1, 1],
    ]
)
weight_table = [1.0 / 3.0] + [1.0 / 18.0] * 6 + [1.0 / 36.0] * 12
opposite_table = [0, 2, 1, 4, 3, 6, 5, 8, 7, 10, 9, 12, 11, 14, 13, 16, 15, 18, 17]
stress_pairs = [(0, 0), (1, 1), (2, 2), (0, 1), (0, 2), (1, 2)]
tau_base = 0.55
smag_term = 18.0 * 1.4142135623730951 * 0.17 * 0.17
regular_eps = 0.0001
stiffness = 2.0
far_velocity = (0.02, 0.06, 0.0)
MESH = pl.DeviceIdType.MESH
f32 = jnp.float32
bf16 = jnp.bfloat16
i32 = jnp.int32

facing = [
    {sign: [q for q in range(19) if velocity_table[q][axis] == sign] for sign in (1, -1)}
    for axis in range(3)
]
Z_SIDES = ((0, 0), (1, 0), (-1, 0), (0, 1), (0, -1))
Y_SIDES = (0, 1, -1)


def project(direction, vector):
    projection = None
    for component in range(3):
        lattice_step = int(velocity_table[direction][component])
        if lattice_step != 0:
            term = vector[component] if lattice_step == 1 else -vector[component]
            projection = term if projection is None else projection + term
    return projection


def moments(populations):
    density = populations[0]
    momentum = [None, None, None]
    for direction in range(1, 19):
        density = density + populations[direction]
        for component in range(3):
            lattice_step = int(velocity_table[direction][component])
            if lattice_step != 0:
                term = populations[direction] if lattice_step == 1 else -populations[direction]
                momentum[component] = (
                    term if momentum[component] is None else momentum[component] + term
                )
    return (density, momentum)


def equilibrium(density, velocity):
    speed_sq = velocity[0] * velocity[0] + velocity[1] * velocity[1] + velocity[2] * velocity[2]
    base = 1.0 - 1.5 * speed_sq
    result = []
    for direction in range(19):
        projected = project(direction, velocity)
        inner = base if projected is None else base + projected * (3.0 + 4.5 * projected)
        result.append(weight_table[direction] * density * inner)
    return result


def far_field():
    speed_sq = sum(v * v for v in far_velocity)
    values = []
    for direction in range(19):
        projected = sum(int(velocity_table[direction][i]) * far_velocity[i] for i in range(3))
        values.append(
            weight_table[direction]
            * (1.0 + 3.0 * projected + 4.5 * projected * projected - 1.5 * speed_sq)
        )
    return values


def collide(populations, cell_force, solid):
    density, momentum = moments(populations)
    inverse = 1.0 / density
    velocity = [
        (momentum[component] + 0.5 * cell_force[component]) * inverse for component in range(3)
    ]
    balance = equilibrium(density, velocity)
    stress = [None] * 6
    departure = []
    for direction in range(19):
        non_eq = populations[direction] - balance[direction]
        departure.append(non_eq)
        for pair_pos in range(6):
            row_axis, col_axis = stress_pairs[pair_pos]
            factor = int(velocity_table[direction][row_axis] * velocity_table[direction][col_axis])
            if factor != 0:
                term = non_eq if factor == 1 else -non_eq
                stress[pair_pos] = term if stress[pair_pos] is None else stress[pair_pos] + term
    shear_sq = stress[0] * stress[0] + stress[1] * stress[1] + stress[2] * stress[2]
    shear_sq = shear_sq + 2.0 * (
        stress[3] * stress[3] + stress[4] * stress[4] + stress[5] * stress[5]
    )
    magnitude = jnp.sqrt(shear_sq + regular_eps)
    relax_time = 0.5 * (tau_base + jnp.sqrt(tau_base * tau_base + smag_term * magnitude * inverse))
    rate = 1.0 / relax_time
    guo_factor = 1.0 - 0.5 * rate
    speed_force = (
        velocity[0] * cell_force[0] + velocity[1] * cell_force[1] + velocity[2] * cell_force[2]
    )
    base = -3.0 * speed_force
    result = []
    for direction in range(19):
        along_force = project(direction, cell_force)
        along_speed = project(direction, velocity)
        inner = base if along_force is None else base + along_force * (3.0 + 9.0 * along_speed)
        relaxed = (
            populations[direction]
            - departure[direction] * rate
            + (guo_factor * weight_table[direction]) * inner
        )
        result.append(jnp.where(solid, populations[opposite_table[direction]], relaxed))
    return result


def pick_rows(one_hot, values):
    high = values.astype(bf16)
    rest = values - high.astype(f32)
    middle = rest.astype(bf16)
    low = (rest - middle.astype(f32)).astype(bf16)
    pieces = jnp.concatenate([low, middle, high], axis=1)
    found = jnp.dot(one_hot, pieces, preferred_element_type=f32)
    n = values.shape[1]
    return found[:, :n] + found[:, n : 2 * n] + found[:, 2 * n :]


def iota(shape, dim):
    return lax.broadcasted_iota(i32, shape, dim)


def hot(condition):
    return jnp.where(condition, 1.0, 0.0).astype(bf16)


def to_column(row):
    n = row.shape[1]
    square = jnp.broadcast_to(row, (n, n))
    return jnp.sum(jnp.where(iota((n, n), 0) == iota((n, n), 1), square, 0.0), axis=1, keepdims=True)


def kernel(
    px,
    py,
    pz,
    pop_in,
    solid_in,
    cells_in,
    weights_in,
    owner_in,
    block_in,
    train_in,
    area_in,
    speed_in,
    out,
    force_out,
    pop,
    solid,
    cells,
    weights,
    owner,
    block,
    train,
    area,
    speed,
    table,
    rows,
    place,
    place_t,
    combine,
    combine_t,
    lab_send,
    lab_recv,
    z_send,
    z_recv,
    d_send,
    d_recv,
    f_all,
    r_send,
    r_recv,
    point_hot,
    cell_force,
    relaxed,
    x_send,
    x_recv,
    y_send,
    y_recv,
    t_send,
    t_recv,
    send_sem,
    recv_sem,
    halo_send,
    halo_recv,
    load_sem,
):
    slots, kern, mark = cells.shape
    size_x, size_y, size_z = pop.shape[1:]
    own = area.shape[0]
    cap = 2
    per_plane = py * cap
    total_rows = px * per_plane
    row_count = size_x * size_y
    gx, gy, gz = lax.axis_index("gx"), lax.axis_index("gy"), lax.axis_index("gz")

    def at(dx, dy, dz):
        return (
            lax.rem(gx + px + dx, px),
            lax.rem(gy + py + dy, py),
            lax.rem(gz + pz + dz, pz),
        )

    halo_far = (
        [(0, 0, s) for s in (1, -1)]
        + [(a, b, 0) for a in (1, -1) for b in (1, -1)]
        + [(a, 0, b) for a in (1, -1) for b in (1, -1)]
        + [(0, a, b) for a in (1, -1) for b in (1, -1)]
    )
    loads = [
        pltpu.make_async_copy(source, target, load_sem.at[n])
        for n, (source, target) in enumerate(
            (
                (owner_in, owner),
                (block_in, block),
                (pop_in, pop),
                (cells_in, cells),
                (weights_in, weights),
                (train_in, train),
                (area_in, area),
                (speed_in, speed),
                (solid_in, solid),
            )
        )
    ]
    for load in loads:
        load.start()
    barrier = pltpu.get_barrier_semaphore()

    def greet_x(k, _):
        pl.semaphore_signal(barrier, inc=1, device_id=at(k, 0, 0), device_id_type=MESH)
        return 0

    def greet_y(k, _):
        pl.semaphore_signal(barrier, inc=1, device_id=at(0, k, 0), device_id_type=MESH)
        return 0

    lax.fori_loop(1, px, greet_x, 0)
    lax.fori_loop(1, py, greet_y, 0)
    for place_of in halo_far:
        pl.semaphore_signal(barrier, inc=1, device_id=at(*place_of), device_id_type=MESH)

    loads[0].wait()
    loads[1].wait()
    owner_row = owner[...].astype(f32)
    owner_col = to_column(owner_row)
    same = owner_col == owner_row
    first, second = iota((slots, slots), 0), iota((slots, slots), 1)
    rank_row = jnp.sum(jnp.where(same & (first < second), 1.0, 0.0), axis=0, keepdims=True)
    rank_col = jnp.sum(jnp.where(same & (second < first), 1.0, 0.0), axis=1, keepdims=True)
    target_row = (owner_row * cap + rank_row).astype(i32)
    target_col = (owner_col * cap + rank_col).astype(i32)
    place[...] = hot(iota((total_rows, slots), 0) == target_row)
    place_t[...] = hot(iota((slots, total_rows), 1) == target_col)
    label_col = to_column(block[...].astype(f32)) + 1.0
    half = mark // per_plane
    plane_hot = hot(iota((px, slots), 0) == target_row // per_plane)
    spot = lax.rem(target_col, per_plane) + per_plane * lax.rem(gx, half)
    label_hot = jnp.where(iota((slots, mark), 1) == spot, label_col, 0.0).astype(bf16)
    labels = jnp.dot(plane_hot, label_hot, preferred_element_type=f32)
    for n in range(px):
        lab_send[n] = labels[n : n + 1]
    lab_recv[gx] = lab_send[gx]

    loads[2].wait()
    density, momentum = moments([pop[q] for q in range(19)])
    for c in range(3):
        table[c] = (momentum[c] / density).reshape(row_count, size_z)


    def send_x(source, target, stage):
        def step(i, _):
            k = px // 2 + ((i + 1) // 2) * (1 - 2 * lax.rem(i, 2))
            peer = at(k, 0, 0)
            pltpu.make_async_remote_copy(
                src_ref=source.at[peer[0]],
                dst_ref=target.at[gx],
                send_sem=send_sem.at[stage],
                recv_sem=recv_sem.at[stage],
                device_id=peer,
                device_id_type=MESH,
            ).start()
            return 0

        lax.fori_loop(0, px - 1, step, 0)

    def send_y(source, own_place, target, stage):
        def step(i, _):
            k = py // 2 + ((i + 1) // 2) * (1 - 2 * lax.rem(i, 2))
            peer = at(0, k, 0)
            pltpu.make_async_remote_copy(
                src_ref=source.at[gy if own_place else peer[1]],
                dst_ref=target.at[gy],
                send_sem=send_sem.at[stage],
                recv_sem=recv_sem.at[stage],
                device_id=peer,
                device_id_type=MESH,
            ).start()
            return 0

        lax.fori_loop(0, py - 1, step, 0)

    def wait_for(buffer, count, semaphore):
        part = buffer.at[pl.ds(0, count)]
        pltpu.make_async_copy(part, part, semaphore).wait()

    LAB, ZS, DS, FS, RS = 0, 1, 4, 7, 10

    def gather(c):
        def step(s, _):
            index = cells[s]
            lane = index & (size_z - 1)
            line = index // size_z
            found = jnp.zeros((kern, mark), f32)
            for h in range(row_count):
                entry = jnp.broadcast_to(table[c, h : h + 1, :], (kern, size_z))
                found = jnp.where(line == h, jnp.take_along_axis(entry, lane, axis=1), found)
            rows[c, pl.ds(s, 1), :] = jnp.sum(found * weights[s], axis=0, keepdims=True)
            return 0

        lax.fori_loop(0, slots, step, 0, unroll=8)

    def send_rows(c):
        z_send[c] = pick_rows(place[...], rows[c]).reshape(px, per_plane, mark)
        z_recv[c, gx] = z_send[c, gx]
        send_x(z_send.at[c], z_recv.at[c], ZS + c)

    def read_labels():
        wait_for(lab_recv, px - 1, recv_sem.at[LAB])
        parts, columns = [], []
        for n in range(total_rows // mark):
            label = jnp.sum(lab_recv[n * half : (n + 1) * half], axis=0)
            group = lax.rem(iota((1, mark), 1), per_plane) // cap
            key = jnp.where(label > 0.5, group.astype(f32) * own + label - 1.0, -1.0)
            parts.append(key)
            columns.append(to_column(key))
        key_row = jnp.concatenate(parts, axis=1).astype(i32)
        key_col = jnp.concatenate(columns, axis=0).astype(i32)
        combine[...] = hot(iota((py * own, total_rows), 0) == key_row)
        combine_t[...] = hot(iota((total_rows, py * own), 1) == key_col)

    def send_sums(c):
        wait_for(z_recv.at[c], px - 1, recv_sem.at[ZS + c])
        d_send[c] = pick_rows(combine[...], z_recv[c].reshape(total_rows, mark)).reshape(
            py, own, mark
        )
        d_recv[c, gy] = d_send[c, gy]
        send_y(d_send.at[c], False, d_recv.at[c], DS + c)

    for load in loads[5:]:
        load.wait()
    train_col = to_column(train[...].astype(f32))

    def send_force(c):
        wait_for(d_recv.at[c], py - 1, recv_sem.at[DS + c])
        marker_velocity = d_recv[c, 0]
        for n in range(1, py):
            marker_velocity = marker_velocity + d_recv[c, n]
        goal = jnp.zeros((own, 1), f32)
        for t in range(speed.shape[0]):
            goal = jnp.where(train_col == float(t), speed[t, c], goal)
        force = stiffness * area[...] * (goal - marker_velocity)
        force_out[c] = force
        f_all[c, gy] = force
        send_y(f_all.at[c], True, f_all.at[c], FS + c)

    def make_back(c):
        wait_for(f_all.at[c], py - 1, recv_sem.at[FS + c])
        r_send[c] = pick_rows(combine_t[...], f_all[c].reshape(py * own, mark)).reshape(
            px, per_plane, mark
        )
        r_recv[c, gx] = r_send[c, gx]

    def send_back(c):
        send_x(r_send.at[c], r_recv.at[c], RS + c)

    def point_one_hots(begin, end):
        def step(s, _):
            lane = (cells[s] & (size_z - 1)).astype(f32)
            columns = jnp.transpose(jnp.concatenate([lane] * (mark // kern), axis=0))
            place_of = iota((mark, size_z), 1).astype(f32).astype(bf16)
            for k in range(kern):
                wanted = jnp.broadcast_to(columns[:, k : k + 1], (mark, size_z)).astype(bf16)
                point_hot[s, k * mark : (k + 1) * mark, :] = jnp.where(
                    wanted == place_of, bf16(1), bf16(0)
                )
            return 0

        lax.fori_loop(begin, end, step, 0, unroll=4)

    def spread(c):
        wait_for(r_recv.at[c], px - 1, recv_sem.at[RS + c])
        rows[c] = pick_rows(place_t[...], r_recv[c].reshape(total_rows, mark))

        def step(s, total):
            line = (cells[s] // size_z).astype(f32)
            value = weights[s] * rows[c, pl.ds(s, 1), :]
            high = value.astype(bf16).astype(f32)
            low = value - high
            zero = bf16(0)
            columns = []
            for k in range(kern):
                wanted = jnp.broadcast_to(line[k : k + 1, :], (16, mark)).astype(bf16)
                pieces = []
                for piece in (high, low):
                    spread_piece = jnp.broadcast_to(piece[k : k + 1, :], (16, mark)).astype(bf16)
                    for j in range(row_count // 16):
                        place_of = (iota((16, mark), 0) + 16 * j).astype(f32).astype(bf16)
                        pieces.append(jnp.where(wanted == place_of, spread_piece, zero))
                columns.append(jnp.concatenate(pieces, axis=0))
            return total + jnp.dot(
                jnp.concatenate(columns, axis=1), point_hot[s], preferred_element_type=f32
            )

        total = lax.fori_loop(
            0, slots, step, jnp.zeros((2 * row_count, size_z), f32), unroll=16
        )
        cell_force[c] = (total[:row_count] + total[row_count:]).reshape(size_x, size_y, size_z)

    loads[3].wait()
    loads[4].wait()
    gather(0)
    pl.semaphore_wait(barrier, px - 1 + py - 1 + len(halo_far))
    send_x(lab_send, lab_recv, LAB)
    send_rows(0)
    gather(1)
    send_rows(1)
    read_labels()
    gather(2)
    send_rows(2)
    send_sums(0)
    point_one_hots(0 * slots // 4, 1 * slots // 4)
    send_force(0)
    send_sums(1)
    point_one_hots(1 * slots // 4, 2 * slots // 4)
    point_one_hots(2 * slots // 4, 3 * slots // 4)
    make_back(0)
    send_sums(2)
    send_back(0)
    send_force(1)
    point_one_hots(3 * slots // 4, 4 * slots // 4)
    make_back(1)
    send_back(1)
    send_force(2)
    make_back(2)
    send_back(2)
    spread(0)
    spread(1)
    spread(2)

    def relax(x):
        result = collide(
            [pop[q, x] for q in range(19)], [cell_force[c, x] for c in range(3)], solid[x] == 1
        )
        for q in range(19):
            relaxed[q, x] = result[q]

    lane_at = iota((size_y, size_z), 1)
    line_at = iota((size_y, size_z), 0)
    halo = []

    def send_halo(source, target, place_of):
        n = len(halo)
        copy = pltpu.make_async_remote_copy(
            src_ref=source,
            dst_ref=target,
            send_sem=halo_send.at[n],
            recv_sem=halo_recv.at[n],
            device_id=at(*place_of),
            device_id_type=MESH,
        )
        copy.start()
        halo.append(copy)

    relax(0)
    relax(size_x - 1)
    for d, sign in enumerate((1, -1)):
        edge = size_x - 1 if sign == 1 else 0
        for n, q in enumerate(facing[0][sign]):
            x_send[d, n] = relaxed[q, edge]
        send_halo(x_send.at[d], x_recv.at[d], (sign, 0, 0))
    for x in range(1, size_x - 1):
        relax(x)
    for d, sign in enumerate((1, -1)):
        tile = jnp.zeros((size_y, size_z), f32)
        edge = size_z - 1 if sign == 1 else 0
        for n, q in enumerate(facing[2][sign]):
            for x in range(size_x):
                column = jnp.broadcast_to(relaxed[q, x][:, edge : edge + 1], (size_y, size_z))
                tile = jnp.where(lane_at == n * size_x + x, column, tile)
        t_send[d] = tile
        for side, (dx, dy) in reversed(list(enumerate(Z_SIDES))):
            send_halo(t_send.at[d], t_recv.at[d, side], (dx, dy, sign))
    for d, sign in enumerate((1, -1)):
        edge = size_y - 1 if sign == 1 else 0
        for n, q in enumerate(facing[1][sign]):
            y_send[d, n * size_x : (n + 1) * size_x, :] = relaxed[q, :, edge, :]
        for side, dx in reversed(list(enumerate(Y_SIDES))):
            send_halo(y_send.at[d], y_recv.at[d, side], (dx, sign, 0))
    for copy in halo:
        copy.wait_recv()

    on_side = (
        ((line_at == 0) & (gy == 0))
        | ((line_at == size_y - 1) & (gy == py - 1))
        | ((lane_at == 0) & (gz == 0))
        | ((lane_at == size_z - 1) & (gz == pz - 1))
    )
    far = far_field()
    for q in range(19):
        cx, cy, cz = (int(v) for v in velocity_table[q])
        for x in range(size_x):
            source = x - cx
            inside = 0 <= source < size_x
            at_edge = source % size_x
            if inside:
                plane = relaxed[q, source]
            else:
                plane = x_recv[0 if cx == 1 else 1, facing[0][cx].index(q)]
            side = 0 if inside else (1 if cx == 1 else 2)
            if cy != 0:
                d = 0 if cy == 1 else 1
                n = facing[1][cy].index(q) * size_x + at_edge
                row = jnp.broadcast_to(y_recv[d, side, n : n + 1, :], (size_y, size_z))
                plane = pltpu.roll(plane, cy % size_y, 0)
                plane = jnp.where(line_at == (0 if cy == 1 else size_y - 1), row, plane)
            if cz != 0:
                d = 0 if cz == 1 else 1
                n = facing[2][cz].index(q) * size_x + at_edge
                tile = t_recv[d, side]
                if cy != 0:
                    beside = pltpu.roll(t_recv[d, 3 if cy == 1 else 4], cy % size_y, 0)
                    tile = pltpu.roll(tile, cy % size_y, 0)
                    tile = jnp.where(line_at == (0 if cy == 1 else size_y - 1), beside, tile)
                column = jnp.broadcast_to(tile[:, n : n + 1], (size_y, size_z))
                plane = pltpu.roll(plane, cz % size_z, 1)
                plane = jnp.where(lane_at == (0 if cz == 1 else size_z - 1), column, plane)
            out[q, x] = jnp.where(on_side, f32(far[q]), plane)

    wait_for(lab_send, px - 1, send_sem.at[LAB])
    for c in range(3):
        wait_for(z_send.at[c], px - 1, send_sem.at[ZS + c])
        wait_for(d_send.at[c], py - 1, send_sem.at[DS + c])
        wait_for(f_all.at[c], py - 1, send_sem.at[FS + c])
        wait_for(r_send.at[c], px - 1, send_sem.at[RS + c])
    for copy in halo:
        copy.wait_send()


def per_device(
    populations,
    solid_cells,
    slot_cells,
    slot_weights,
    slot_owner,
    slot_block,
    train_of_block,
    marker_area,
    train_velocity,
):
    px, py, pz = (lax.axis_size(axis) for axis in ("gx", "gy", "gz"))
    slots, kern, mark = slot_cells.shape[3:]
    own = train_of_block.shape[3]
    _, size_x, size_y, size_z = populations.shape
    rows_out = px * py * 2
    vmem = pl.BlockSpec(memory_space=pltpu.VMEM)
    hbm = pl.BlockSpec(memory_space=pltpu.HBM)
    face = 5 * size_x
    face_rows = -(-face // 8) * 8
    scratch = [
        pltpu.VMEM(populations.shape, f32),
        pltpu.VMEM(solid_cells.shape, i32),
        pltpu.VMEM((slots, kern, mark), i32),
        pltpu.VMEM((slots, kern, mark), f32),
        pltpu.VMEM((1, slots), i32),
        pltpu.VMEM((1, slots), i32),
        pltpu.VMEM((1, own), i32),
        pltpu.VMEM((own, mark), f32),
        pltpu.SMEM(train_velocity.shape, f32),
        pltpu.VMEM((3, size_x * size_y, size_z), f32),
        pltpu.VMEM((3, slots, mark), f32),
        pltpu.VMEM((rows_out, slots), bf16),
        pltpu.VMEM((slots, rows_out), bf16),
        pltpu.VMEM((py * own, rows_out), bf16),
        pltpu.VMEM((rows_out, py * own), bf16),
        pltpu.VMEM((px, 1, mark), f32),
        pltpu.VMEM((px, 1, mark), f32),
        pltpu.VMEM((3, px, py * 2, mark), f32),
        pltpu.VMEM((3, px, py * 2, mark), f32),
        pltpu.VMEM((3, py, own, mark), f32),
        pltpu.VMEM((3, py, own, mark), f32),
        pltpu.VMEM((3, py, own, mark), f32),
        pltpu.VMEM((3, px, py * 2, mark), f32),
        pltpu.VMEM((3, px, py * 2, mark), f32),
        pltpu.VMEM((slots, kern * mark, size_z), bf16),
        pltpu.VMEM((3, size_x, size_y, size_z), f32),
        pltpu.VMEM((19, size_x, size_y, size_z), f32),
        pltpu.VMEM((2, 5, size_y, size_z), f32),
        pltpu.VMEM((2, 5, size_y, size_z), f32),
        pltpu.VMEM((2, face_rows, size_z), f32),
        pltpu.VMEM((2, 3, face_rows, size_z), f32),
        pltpu.VMEM((2, size_y, size_z), f32),
        pltpu.VMEM((2, 5, size_y, size_z), f32),
        pltpu.SemaphoreType.DMA((13,)),
        pltpu.SemaphoreType.DMA((13,)),
        pltpu.SemaphoreType.DMA((18,)),
        pltpu.SemaphoreType.DMA((18,)),
        pltpu.SemaphoreType.DMA((9,)),
    ]
    populations_next, marker_force = pl.pallas_call(
        functools.partial(kernel, px, py, pz),
        out_shape=(
            pltpu.VMEM(populations.shape, f32),
            pltpu.VMEM((3, own, mark), f32),
        ),
        in_specs=[hbm] * 9,
        out_specs=(vmem, vmem),
        scratch_shapes=scratch,
        compiler_params=pltpu.CompilerParams(
            collective_id=0, has_side_effects=True, vmem_limit_bytes=60 << 20
        ),
        name="step",
    )(
        populations,
        solid_cells,
        slot_cells.reshape(slots, kern, mark),
        slot_weights.reshape(slots, kern, mark),
        slot_owner.reshape(1, slots),
        slot_block.reshape(1, slots),
        train_of_block.reshape(1, own),
        marker_area.reshape(own, mark),
        train_velocity,
    )
    return (populations_next, marker_force.transpose(1, 0, 2).reshape(1, 1, 1, own, 3, mark))


def solution(mesh):
    placed = (
        P(None, "gx", "gy", "gz"),
        P("gx", "gy", "gz"),
        P("gx", "gy", "gz", None, None, None),
        P("gx", "gy", "gz", None, None, None),
        P("gx", "gy", "gz", None, None),
        P("gx", "gy", "gz", None),
        P("gx", "gy", "gz", None),
        P("gx", "gy", "gz", None, None),
        P(),
    )
    return jax.shard_map(
        per_device,
        mesh=mesh,
        in_specs=placed,
        out_specs=(P(None, "gx", "gy", "gz"), P("gx", "gy", "gz", None, None, None)),
        check_vma=False,
    )
```

```python
import functools

import jax
import jax.numpy as jnp
import numpy as np
from jax import lax
from jax.experimental import pallas as pl
from jax.experimental.pallas import tpu as pltpu
from jax.sharding import PartitionSpec as P

velocity_table = np.array(
    [
        [0, 0, 0],
        [1, 0, 0],
        [-1, 0, 0],
        [0, 1, 0],
        [0, -1, 0],
        [0, 0, 1],
        [0, 0, -1],
        [1, 1, 0],
        [-1, -1, 0],
        [1, -1, 0],
        [-1, 1, 0],
        [1, 0, 1],
        [-1, 0, -1],
        [1, 0, -1],
        [-1, 0, 1],
        [0, 1, 1],
        [0, -1, -1],
        [0, 1, -1],
        [0, -1, 1],
    ]
)
weight_table = [1.0 / 3.0] + [1.0 / 18.0] * 6 + [1.0 / 36.0] * 12
opposite_table = [0, 2, 1, 4, 3, 6, 5, 8, 7, 10, 9, 12, 11, 14, 13, 16, 15, 18, 17]
stress_pairs = [(0, 0), (1, 1), (2, 2), (0, 1), (0, 2), (1, 2)]
tau_base = 0.55
smag_term = 18.0 * 1.4142135623730951 * 0.17 * 0.17
regular_eps = 0.0001
stiffness = 2.0
far_velocity = (0.02, 0.06, 0.0)
MESH = pl.DeviceIdType.MESH
f32 = jnp.float32
bf16 = jnp.bfloat16
i32 = jnp.int32

facing = [
    {sign: [q for q in range(19) if velocity_table[q][axis] == sign] for sign in (1, -1)}
    for axis in range(3)
]
Z_SIDES = ((0, 0), (1, 0), (-1, 0), (0, 1), (0, -1))
Y_SIDES = (0, 1, -1)


def project(direction, vector):
    projection = None
    for component in range(3):
        lattice_step = int(velocity_table[direction][component])
        if lattice_step != 0:
            term = vector[component] if lattice_step == 1 else -vector[component]
            projection = term if projection is None else projection + term
    return projection


def moments(populations):
    density = populations[0]
    momentum = [None, None, None]
    for direction in range(1, 19):
        density = density + populations[direction]
        for component in range(3):
            lattice_step = int(velocity_table[direction][component])
            if lattice_step != 0:
                term = populations[direction] if lattice_step == 1 else -populations[direction]
                momentum[component] = (
                    term if momentum[component] is None else momentum[component] + term
                )
    return (density, momentum)


def equilibrium(density, velocity):
    speed_sq = velocity[0] * velocity[0] + velocity[1] * velocity[1] + velocity[2] * velocity[2]
    base = 1.0 - 1.5 * speed_sq
    result = []
    for direction in range(19):
        projected = project(direction, velocity)
        inner = base if projected is None else base + projected * (3.0 + 4.5 * projected)
        result.append(weight_table[direction] * density * inner)
    return result


def far_field():
    speed_sq = sum(v * v for v in far_velocity)
    values = []
    for direction in range(19):
        projected = sum(int(velocity_table[direction][i]) * far_velocity[i] for i in range(3))
        values.append(
            weight_table[direction]
            * (1.0 + 3.0 * projected + 4.5 * projected * projected - 1.5 * speed_sq)
        )
    return values


def collide(populations, cell_force, solid):
    density, momentum = moments(populations)
    inverse = 1.0 / density
    velocity = [
        (momentum[component] + 0.5 * cell_force[component]) * inverse for component in range(3)
    ]
    balance = equilibrium(density, velocity)
    stress = [None] * 6
    departure = []
    for direction in range(19):
        non_eq = populations[direction] - balance[direction]
        departure.append(non_eq)
        for pair_pos in range(6):
            row_axis, col_axis = stress_pairs[pair_pos]
            factor = int(velocity_table[direction][row_axis] * velocity_table[direction][col_axis])
            if factor != 0:
                term = non_eq if factor == 1 else -non_eq
                stress[pair_pos] = term if stress[pair_pos] is None else stress[pair_pos] + term
    shear_sq = stress[0] * stress[0] + stress[1] * stress[1] + stress[2] * stress[2]
    shear_sq = shear_sq + 2.0 * (
        stress[3] * stress[3] + stress[4] * stress[4] + stress[5] * stress[5]
    )
    magnitude = jnp.sqrt(shear_sq + regular_eps)
    relax_time = 0.5 * (tau_base + jnp.sqrt(tau_base * tau_base + smag_term * magnitude * inverse))
    rate = 1.0 / relax_time
    guo_factor = 1.0 - 0.5 * rate
    speed_force = (
        velocity[0] * cell_force[0] + velocity[1] * cell_force[1] + velocity[2] * cell_force[2]
    )
    base = -3.0 * speed_force
    result = []
    for direction in range(19):
        along_force = project(direction, cell_force)
        along_speed = project(direction, velocity)
        inner = base if along_force is None else base + along_force * (3.0 + 9.0 * along_speed)
        relaxed = (
            populations[direction]
            - departure[direction] * rate
            + (guo_factor * weight_table[direction]) * inner
        )
        result.append(jnp.where(solid, populations[opposite_table[direction]], relaxed))
    return result


def pick_rows(one_hot, values):
    high = values.astype(bf16)
    rest = values - high.astype(f32)
    middle = rest.astype(bf16)
    low = (rest - middle.astype(f32)).astype(bf16)
    pieces = jnp.concatenate([low, middle, high], axis=1)
    found = jnp.dot(one_hot, pieces, preferred_element_type=f32)
    n = values.shape[1]
    return found[:, :n] + found[:, n : 2 * n] + found[:, 2 * n :]


def iota(shape, dim):
    return lax.broadcasted_iota(i32, shape, dim)


def hot(condition):
    return jnp.where(condition, 1.0, 0.0).astype(bf16)


def to_column(row):
    n = row.shape[1]
    square = jnp.broadcast_to(row, (n, n))
    return jnp.sum(jnp.where(iota((n, n), 0) == iota((n, n), 1), square, 0.0), axis=1, keepdims=True)


def kernel(
    px,
    py,
    pz,
    pop_in,
    solid_in,
    cells_in,
    weights_in,
    owner_in,
    block_in,
    train_in,
    area_in,
    speed_in,
    out,
    force_out,
    pop,
    solid,
    cells,
    weights,
    owner,
    block,
    train,
    area,
    speed,
    table,
    rows,
    place,
    place_t,
    combine,
    combine_t,
    lab_send,
    lab_recv,
    z_send,
    z_recv,
    d_send,
    d_recv,
    f_all,
    r_send,
    r_recv,
    point_hot,
    cell_force,
    relaxed,
    x_send,
    x_recv,
    y_send,
    y_recv,
    t_send,
    t_recv,
    send_sem,
    recv_sem,
    halo_send,
    halo_recv,
    load_sem,
):
    slots, kern, mark = cells.shape
    size_x, size_y, size_z = pop.shape[1:]
    own = area.shape[0]
    cap = 2
    per_plane = py * cap
    total_rows = px * per_plane
    row_count = size_x * size_y
    gx, gy, gz = lax.axis_index("gx"), lax.axis_index("gy"), lax.axis_index("gz")

    def at(dx, dy, dz):
        return (
            lax.rem(gx + px + dx, px),
            lax.rem(gy + py + dy, py),
            lax.rem(gz + pz + dz, pz),
        )

    halo_far = (
        [(0, 0, s) for s in (1, -1)]
        + [(a, b, 0) for a in (1, -1) for b in (1, -1)]
        + [(a, 0, b) for a in (1, -1) for b in (1, -1)]
        + [(0, a, b) for a in (1, -1) for b in (1, -1)]
    )
    loads = [
        pltpu.make_async_copy(source, target, load_sem.at[n])
        for n, (source, target) in enumerate(
            (
                (owner_in, owner),
                (block_in, block),
                (pop_in, pop),
                (cells_in, cells),
                (weights_in, weights),
                (train_in, train),
                (area_in, area),
                (speed_in, speed),
                (solid_in, solid),
            )
        )
    ]
    for load in loads:
        load.start()
    barrier = pltpu.get_barrier_semaphore()

    def greet_x(k, _):
        pl.semaphore_signal(barrier, inc=1, device_id=at(k, 0, 0), device_id_type=MESH)
        return 0

    def greet_y(k, _):
        pl.semaphore_signal(barrier, inc=1, device_id=at(0, k, 0), device_id_type=MESH)
        return 0

    lax.fori_loop(1, px, greet_x, 0)
    lax.fori_loop(1, py, greet_y, 0)
    for place_of in halo_far:
        pl.semaphore_signal(barrier, inc=1, device_id=at(*place_of), device_id_type=MESH)

    loads[0].wait()
    loads[1].wait()
    owner_row = owner[...].astype(f32)
    owner_col = to_column(owner_row)
    same = owner_col == owner_row
    first, second = iota((slots, slots), 0), iota((slots, slots), 1)
    rank_row = jnp.sum(jnp.where(same & (first < second), 1.0, 0.0), axis=0, keepdims=True)
    rank_col = jnp.sum(jnp.where(same & (second < first), 1.0, 0.0), axis=1, keepdims=True)
    target_row = (owner_row * cap + rank_row).astype(i32)
    target_col = (owner_col * cap + rank_col).astype(i32)
    place[...] = hot(iota((total_rows, slots), 0) == target_row)
    place_t[...] = hot(iota((slots, total_rows), 1) == target_col)
    label_col = to_column(block[...].astype(f32)) + 1.0
    half = mark // per_plane
    plane_hot = hot(iota((px, slots), 0) == target_row // per_plane)
    spot = lax.rem(target_col, per_plane) + per_plane * lax.rem(gx, half)
    label_hot = jnp.where(iota((slots, mark), 1) == spot, label_col, 0.0).astype(bf16)
    labels = jnp.dot(plane_hot, label_hot, preferred_element_type=f32)
    for n in range(px):
        lab_send[n] = labels[n : n + 1]
    lab_recv[gx] = lab_send[gx]

    loads[2].wait()
    density, momentum = moments([pop[q] for q in range(19)])
    for c in range(3):
        table[c] = (momentum[c] / density).reshape(row_count, size_z)


    def send_x(source, target, stage):
        def step(i, _):
            k = px // 2 + ((i + 1) // 2) * (1 - 2 * lax.rem(i, 2))
            peer = at(k, 0, 0)
            pltpu.make_async_remote_copy(
                src_ref=source.at[peer[0]],
                dst_ref=target.at[gx],
                send_sem=send_sem.at[stage],
                recv_sem=recv_sem.at[stage],
                device_id=peer,
                device_id_type=MESH,
            ).start()
            return 0

        lax.fori_loop(0, px - 1, step, 0)

    def send_y(source, own_place, target, stage):
        def step(i, _):
            k = py // 2 + ((i + 1) // 2) * (1 - 2 * lax.rem(i, 2))
            peer = at(0, k, 0)
            pltpu.make_async_remote_copy(
                src_ref=source.at[gy if own_place else peer[1]],
                dst_ref=target.at[gy],
                send_sem=send_sem.at[stage],
                recv_sem=recv_sem.at[stage],
                device_id=peer,
                device_id_type=MESH,
            ).start()
            return 0

        lax.fori_loop(0, py - 1, step, 0)

    def wait_for(buffer, count, semaphore):
        part = buffer.at[pl.ds(0, count)]
        pltpu.make_async_copy(part, part, semaphore).wait()

    LAB, ZS, DS, FS, RS = 0, 1, 4, 7, 10

    def gather(c):
        def step(s, _):
            index = cells[s]
            lane = index & (size_z - 1)
            line = index // size_z
            found = jnp.zeros((kern, mark), f32)
            for h in range(row_count):
                entry = jnp.broadcast_to(table[c, h : h + 1, :], (kern, size_z))
                found = jnp.where(line == h, jnp.take_along_axis(entry, lane, axis=1), found)
            rows[c, pl.ds(s, 1), :] = jnp.sum(found * weights[s], axis=0, keepdims=True)
            return 0

        lax.fori_loop(0, slots, step, 0, unroll=8)

    def send_rows(c):
        z_send[c] = pick_rows(place[...], rows[c]).reshape(px, per_plane, mark)
        z_recv[c, gx] = z_send[c, gx]
        send_x(z_send.at[c], z_recv.at[c], ZS + c)

    def read_labels():
        wait_for(lab_recv, px - 1, recv_sem.at[LAB])
        parts, columns = [], []
        for n in range(total_rows // mark):
            label = jnp.sum(lab_recv[n * half : (n + 1) * half], axis=0)
            group = lax.rem(iota((1, mark), 1), per_plane) // cap
            key = jnp.where(label > 0.5, group.astype(f32) * own + label - 1.0, -1.0)
            parts.append(key)
            columns.append(to_column(key))
        key_row = jnp.concatenate(parts, axis=1).astype(i32)
        key_col = jnp.concatenate(columns, axis=0).astype(i32)
        combine[...] = hot(iota((py * own, total_rows), 0) == key_row)
        combine_t[...] = hot(iota((total_rows, py * own), 1) == key_col)

    def send_sums(c):
        wait_for(z_recv.at[c], px - 1, recv_sem.at[ZS + c])
        d_send[c] = pick_rows(combine[...], z_recv[c].reshape(total_rows, mark)).reshape(
            py, own, mark
        )
        d_recv[c, gy] = d_send[c, gy]
        send_y(d_send.at[c], False, d_recv.at[c], DS + c)

    for load in loads[5:]:
        load.wait()
    train_col = to_column(train[...].astype(f32))

    def send_force(c):
        wait_for(d_recv.at[c], py - 1, recv_sem.at[DS + c])
        marker_velocity = d_recv[c, 0]
        for n in range(1, py):
            marker_velocity = marker_velocity + d_recv[c, n]
        goal = jnp.zeros((own, 1), f32)
        for t in range(speed.shape[0]):
            goal = jnp.where(train_col == float(t), speed[t, c], goal)
        force = stiffness * area[...] * (goal - marker_velocity)
        force_out[c] = force
        f_all[c, gy] = force
        send_y(f_all.at[c], True, f_all.at[c], FS + c)

    def make_back(c):
        wait_for(f_all.at[c], py - 1, recv_sem.at[FS + c])
        r_send[c] = pick_rows(combine_t[...], f_all[c].reshape(py * own, mark)).reshape(
            px, per_plane, mark
        )
        r_recv[c, gx] = r_send[c, gx]

    def send_back(c):
        send_x(r_send.at[c], r_recv.at[c], RS + c)

    def point_one_hots(begin, end):
        def step(s, _):
            lane = (cells[s] & (size_z - 1)).astype(f32)
            columns = jnp.transpose(jnp.concatenate([lane] * (mark // kern), axis=0))
            place_of = iota((mark, size_z), 1).astype(f32).astype(bf16)
            for k in range(kern):
                wanted = jnp.broadcast_to(columns[:, k : k + 1], (mark, size_z)).astype(bf16)
                point_hot[s, k * mark : (k + 1) * mark, :] = jnp.where(
                    wanted == place_of, bf16(1), bf16(0)
                )
            return 0

        lax.fori_loop(begin, end, step, 0, unroll=4)

    def spread(c):
        wait_for(r_recv.at[c], px - 1, recv_sem.at[RS + c])
        rows[c] = pick_rows(place_t[...], r_recv[c].reshape(total_rows, mark))

        def step(s, total):
            line = (cells[s] // size_z).astype(f32)
            value = weights[s] * rows[c, pl.ds(s, 1), :]
            high = value.astype(bf16).astype(f32)
            low = value - high
            zero = bf16(0)
            columns = []
            for k in range(kern):
                wanted = jnp.broadcast_to(line[k : k + 1, :], (16, mark)).astype(bf16)
                pieces = []
                for piece in (high, low):
                    spread_piece = jnp.broadcast_to(piece[k : k + 1, :], (16, mark)).astype(bf16)
                    for j in range(row_count // 16):
                        place_of = (iota((16, mark), 0) + 16 * j).astype(f32).astype(bf16)
                        pieces.append(jnp.where(wanted == place_of, spread_piece, zero))
                columns.append(jnp.concatenate(pieces, axis=0))
            return total + jnp.dot(
                jnp.concatenate(columns, axis=1), point_hot[s], preferred_element_type=f32
            )

        total = lax.fori_loop(
            0, slots, step, jnp.zeros((2 * row_count, size_z), f32), unroll=16
        )
        cell_force[c] = (total[:row_count] + total[row_count:]).reshape(size_x, size_y, size_z)

    loads[3].wait()
    loads[4].wait()
    gather(0)
    pl.semaphore_wait(barrier, px - 1 + py - 1 + len(halo_far))
    send_x(lab_send, lab_recv, LAB)
    send_rows(0)
    gather(1)
    send_rows(1)
    gather(2)
    send_rows(2)
    read_labels()
    send_sums(0)
    point_one_hots(0 * slots // 4, 1 * slots // 4)
    send_force(0)
    send_sums(1)
    point_one_hots(1 * slots // 4, 2 * slots // 4)
    point_one_hots(2 * slots // 4, 3 * slots // 4)
    make_back(0)
    send_sums(2)
    send_back(0)
    send_force(1)
    point_one_hots(3 * slots // 4, 4 * slots // 4)
    make_back(1)
    send_back(1)
    send_force(2)
    make_back(2)
    send_back(2)
    spread(0)
    spread(1)
    spread(2)

    def relax(x):
        result = collide(
            [pop[q, x] for q in range(19)], [cell_force[c, x] for c in range(3)], solid[x] == 1
        )
        for q in range(19):
            relaxed[q, x] = result[q]

    lane_at = iota((size_y, size_z), 1)
    line_at = iota((size_y, size_z), 0)
    halo = []

    def send_halo(source, target, place_of):
        n = len(halo)
        copy = pltpu.make_async_remote_copy(
            src_ref=source,
            dst_ref=target,
            send_sem=halo_send.at[n],
            recv_sem=halo_recv.at[n],
            device_id=at(*place_of),
            device_id_type=MESH,
        )
        copy.start()
        halo.append(copy)

    relax(0)
    relax(size_x - 1)
    for d, sign in enumerate((1, -1)):
        edge = size_x - 1 if sign == 1 else 0
        for n, q in enumerate(facing[0][sign]):
            x_send[d, n] = relaxed[q, edge]
        send_halo(x_send.at[d], x_recv.at[d], (sign, 0, 0))
    for x in range(1, size_x - 1):
        relax(x)
    for d, sign in enumerate((1, -1)):
        tile = jnp.zeros((size_y, size_z), f32)
        edge = size_z - 1 if sign == 1 else 0
        for n, q in enumerate(facing[2][sign]):
            for x in range(size_x):
                column = jnp.broadcast_to(relaxed[q, x][:, edge : edge + 1], (size_y, size_z))
                tile = jnp.where(lane_at == n * size_x + x, column, tile)
        t_send[d] = tile
        for side, (dx, dy) in reversed(list(enumerate(Z_SIDES))):
            send_halo(t_send.at[d], t_recv.at[d, side], (dx, dy, sign))
    for d, sign in enumerate((1, -1)):
        edge = size_y - 1 if sign == 1 else 0
        for n, q in enumerate(facing[1][sign]):
            y_send[d, n * size_x : (n + 1) * size_x, :] = relaxed[q, :, edge, :]
        for side, dx in reversed(list(enumerate(Y_SIDES))):
            send_halo(y_send.at[d], y_recv.at[d, side], (dx, sign, 0))
    for copy in halo:
        copy.wait_recv()

    on_side = (
        ((line_at == 0) & (gy == 0))
        | ((line_at == size_y - 1) & (gy == py - 1))
        | ((lane_at == 0) & (gz == 0))
        | ((lane_at == size_z - 1) & (gz == pz - 1))
    )
    far = far_field()
    for q in range(19):
        cx, cy, cz = (int(v) for v in velocity_table[q])
        for x in range(size_x):
            source = x - cx
            inside = 0 <= source < size_x
            at_edge = source % size_x
            if inside:
                plane = relaxed[q, source]
            else:
                plane = x_recv[0 if cx == 1 else 1, facing[0][cx].index(q)]
            side = 0 if inside else (1 if cx == 1 else 2)
            if cy != 0:
                d = 0 if cy == 1 else 1
                n = facing[1][cy].index(q) * size_x + at_edge
                row = jnp.broadcast_to(y_recv[d, side, n : n + 1, :], (size_y, size_z))
                plane = pltpu.roll(plane, cy % size_y, 0)
                plane = jnp.where(line_at == (0 if cy == 1 else size_y - 1), row, plane)
            if cz != 0:
                d = 0 if cz == 1 else 1
                n = facing[2][cz].index(q) * size_x + at_edge
                tile = t_recv[d, side]
                if cy != 0:
                    beside = pltpu.roll(t_recv[d, 3 if cy == 1 else 4], cy % size_y, 0)
                    tile = pltpu.roll(tile, cy % size_y, 0)
                    tile = jnp.where(line_at == (0 if cy == 1 else size_y - 1), beside, tile)
                column = jnp.broadcast_to(tile[:, n : n + 1], (size_y, size_z))
                plane = pltpu.roll(plane, cz % size_z, 1)
                plane = jnp.where(lane_at == (0 if cz == 1 else size_z - 1), column, plane)
            out[q, x] = jnp.where(on_side, f32(far[q]), plane)

    wait_for(lab_send, px - 1, send_sem.at[LAB])
    for c in range(3):
        wait_for(z_send.at[c], px - 1, send_sem.at[ZS + c])
        wait_for(d_send.at[c], py - 1, send_sem.at[DS + c])
        wait_for(f_all.at[c], py - 1, send_sem.at[FS + c])
        wait_for(r_send.at[c], px - 1, send_sem.at[RS + c])
    for copy in halo:
        copy.wait_send()


def per_device(
    populations,
    solid_cells,
    slot_cells,
    slot_weights,
    slot_owner,
    slot_block,
    train_of_block,
    marker_area,
    train_velocity,
):
    px, py, pz = (lax.axis_size(axis) for axis in ("gx", "gy", "gz"))
    slots, kern, mark = slot_cells.shape[3:]
    own = train_of_block.shape[3]
    _, size_x, size_y, size_z = populations.shape
    rows_out = px * py * 2
    vmem = pl.BlockSpec(memory_space=pltpu.VMEM)
    hbm = pl.BlockSpec(memory_space=pltpu.HBM)
    face = 5 * size_x
    face_rows = -(-face // 8) * 8
    scratch = [
        pltpu.VMEM(populations.shape, f32),
        pltpu.VMEM(solid_cells.shape, i32),
        pltpu.VMEM((slots, kern, mark), i32),
        pltpu.VMEM((slots, kern, mark), f32),
        pltpu.VMEM((1, slots), i32),
        pltpu.VMEM((1, slots), i32),
        pltpu.VMEM((1, own), i32),
        pltpu.VMEM((own, mark), f32),
        pltpu.SMEM(train_velocity.shape, f32),
        pltpu.VMEM((3, size_x * size_y, size_z), f32),
        pltpu.VMEM((3, slots, mark), f32),
        pltpu.VMEM((rows_out, slots), bf16),
        pltpu.VMEM((slots, rows_out), bf16),
        pltpu.VMEM((py * own, rows_out), bf16),
        pltpu.VMEM((rows_out, py * own), bf16),
        pltpu.VMEM((px, 1, mark), f32),
        pltpu.VMEM((px, 1, mark), f32),
        pltpu.VMEM((3, px, py * 2, mark), f32),
        pltpu.VMEM((3, px, py * 2, mark), f32),
        pltpu.VMEM((3, py, own, mark), f32),
        pltpu.VMEM((3, py, own, mark), f32),
        pltpu.VMEM((3, py, own, mark), f32),
        pltpu.VMEM((3, px, py * 2, mark), f32),
        pltpu.VMEM((3, px, py * 2, mark), f32),
        pltpu.VMEM((slots, kern * mark, size_z), bf16),
        pltpu.VMEM((3, size_x, size_y, size_z), f32),
        pltpu.VMEM((19, size_x, size_y, size_z), f32),
        pltpu.VMEM((2, 5, size_y, size_z), f32),
        pltpu.VMEM((2, 5, size_y, size_z), f32),
        pltpu.VMEM((2, face_rows, size_z), f32),
        pltpu.VMEM((2, 3, face_rows, size_z), f32),
        pltpu.VMEM((2, size_y, size_z), f32),
        pltpu.VMEM((2, 5, size_y, size_z), f32),
        pltpu.SemaphoreType.DMA((13,)),
        pltpu.SemaphoreType.DMA((13,)),
        pltpu.SemaphoreType.DMA((18,)),
        pltpu.SemaphoreType.DMA((18,)),
        pltpu.SemaphoreType.DMA((9,)),
    ]
    populations_next, marker_force = pl.pallas_call(
        functools.partial(kernel, px, py, pz),
        out_shape=(
            pltpu.VMEM(populations.shape, f32),
            pltpu.VMEM((3, own, mark), f32),
        ),
        in_specs=[hbm] * 9,
        out_specs=(vmem, vmem),
        scratch_shapes=scratch,
        compiler_params=pltpu.CompilerParams(
            collective_id=0, has_side_effects=True, vmem_limit_bytes=60 << 20
        ),
        name="step",
    )(
        populations,
        solid_cells,
        slot_cells.reshape(slots, kern, mark),
        slot_weights.reshape(slots, kern, mark),
        slot_owner.reshape(1, slots),
        slot_block.reshape(1, slots),
        train_of_block.reshape(1, own),
        marker_area.reshape(own, mark),
        train_velocity,
    )
    return (populations_next, marker_force.transpose(1, 0, 2).reshape(1, 1, 1, own, 3, mark))


def solution(mesh):
    placed = (
        P(None, "gx", "gy", "gz"),
        P("gx", "gy", "gz"),
        P("gx", "gy", "gz", None, None, None),
        P("gx", "gy", "gz", None, None, None),
        P("gx", "gy", "gz", None, None),
        P("gx", "gy", "gz", None),
        P("gx", "gy", "gz", None),
        P("gx", "gy", "gz", None, None),
        P(),
    )
    return jax.shard_map(
        per_device,
        mesh=mesh,
        in_specs=placed,
        out_specs=(P(None, "gx", "gy", "gz"), P("gx", "gy", "gz", None, None, None)),
        check_vma=False,
    )
```
